512 devices in a mesh: leaf: 128 (over z, y, core), list: 4 (over x).
Axes of the slice: x: 4, y: 4, z: 16, core: 2. Of those that a mesh axis runs over, the one named last changes fastest.
Arguments:
- charge: float32 [256, 32768], P('list', 'leaf'), may hold values from -3 to 3
- position: float32 [3, 256, 32768], P(None, 'list', 'leaf'), may hold values from -1 to 1
- charge_count: int32 [32768], P('leaf'), may hold values from 0 to 256, as said below
- octant: int32 [36864], P('leaf'), may hold values from 0 to 7, as said below
- shift_ops: bfloat16 [8, 28672], replicated, may hold values from -0.15625 to 0.15625
- m2l_ops: bfloat16 [160, 28672], P('list'), may hold values from -0.0390625 to 0.0390625
- let_send: int32 [128, 8, 128], P('leaf'), may hold values from 0 to 255
- list_src: int32 [128, 160, 384], P('leaf', 'list'), may hold values from 0 to 1279, as said below
- list_dst: int32 [128, 160, 384], P('leaf', 'list'), may hold values from 0 to 255
- batch_count: int32 [128, 160], P('leaf', 'list'), may hold values from 192 to 384, as said below
Outputs:
- local_field: bfloat16 [169, 32768], P(None, ('leaf', 'list'))
- tree_multipoles: bfloat16 [169, 4608], P(None, 'leaf')
The draws below stay inside these ranges and needn't reach their ends.
Inputs may be any that keep to these rules, and one draw needn't show every extreme that they name: `charge_count`: the first leaf of each index of leaf has 256 occupied slots. `octant`: each aligned group of 8 entries is a permutation of 0 to 7. `list_src`: a column 256 + k * 128 + c is used only where d + off(k) is an index of leaf. `batch_count`: every index of leaf has one full batch.
All inputs are finite; a program needn't handle non-finite values.
Results may differ from the reference program's by a relative error of at most 0.0051.
Values may be sent and summed in bfloat16 or wider, within the bound.
A program may use at most 64 MiB of HBM per device.

```python
import math
import jax
import jax.numpy as jnp
import numpy as np
from jax import lax

ORDER = 12
NCOEF = 169
OPW = 28672
PER_LEAF = 256
LEAF_DEV = 256
LEAVES = 32768
TREE_DEV = 36
REACH = 4
CAP = 128
OPS_DEV = 40
NOPS = 160
BATCH = 384
N_LEAF = 128


def draw_charge_count(key, part):
    key = jax.random.fold_in(key, 2)
    counts = jax.random.randint(key, (LEAVES,), 0, PER_LEAF + 1)
    first = jnp.arange(LEAVES) % LEAF_DEV == 0
    return jnp.where(first, PER_LEAF, counts).astype(jnp.int32)


def draw_octant(key, part):
    key = jax.random.fold_in(key, 1)
    total = (LEAF_DEV + LEAF_DEV // 8) * N_LEAF
    scores = jax.random.randint(key, (total // 8, 8), 0, 1 << 20) * 8 + jnp.arange(8)[None, :]
    return jnp.argsort(scores, axis=1, stable=True).reshape(-1).astype(jnp.int32)


def draw_list_src(key, part):
    key = jax.random.fold_in(key, 3)
    upper = LEAF_DEV + 2 * REACH * CAP
    picks = jax.random.randint(key, (N_LEAF, NOPS, BATCH), 0, upper)
    device = jnp.arange(N_LEAF)[:, None, None]
    near_k = (picks - LEAF_DEV) // CAP
    offset = jnp.where(near_k < REACH, near_k - REACH, near_k - REACH + 1)
    sender = device + offset
    outside = (picks >= LEAF_DEV) & ((sender < 0) | (sender >= N_LEAF))
    return jnp.where(outside, picks % LEAF_DEV, picks).astype(jnp.int32)


def draw_batch_count(key, part):
    key = jax.random.fold_in(key, 4)
    counts = jax.random.randint(key, (N_LEAF, NOPS), BATCH // 2, BATCH + 1)
    first = jnp.arange(NOPS)[None, :] == 0
    return jnp.where(first, BATCH, counts).astype(jnp.int32)


def place_ends(result, own_key, smallest, high):
    spot = [jax.random.randint(jax.random.fold_in(own_key, axis), (), 0, length) for axis, length in enumerate(result.shape)]
    widest = result.shape.index(max(result.shape))
    neighbour = spot[:widest] + [(spot[widest] + 1) % result.shape[widest]] + spot[widest + 1:]
    return result.at[tuple(spot)].set(smallest).at[tuple(neighbour)].set(high)


def shard_levels(own_key, shape, split, least, top_value):
    loudness = 1.0
    for dim, parts in split:
        heights = jax.random.uniform(jax.random.fold_in(jax.random.fold_in(own_key, 6), dim), (parts,), jnp.float32, least / len(split), top_value / len(split))
        loudness = loudness * jnp.repeat(jnp.exp(heights), shape[dim] // parts).reshape((-1,) + (1,) * (len(shape) - 1 - dim))
    return loudness


def normal_values(own_key, shape, scale, limit, cuts=(), held_as=jnp.bfloat16):
    factor_of = shard_levels(own_key, shape, cuts, -0.22, 0.18) if cuts else 1.0
    values = jax.random.normal(own_key, shape, jnp.float32) * scale * factor_of
    return jnp.minimum(jnp.maximum(values, -limit), limit).astype(held_as)


def setup_inputs(seed: int = 0) -> dict:
    seeds = jax.random.split(jax.random.key(seed), 11)
    return {
        "charge": normal_values(seeds[0], (PER_LEAF, LEAVES), 0.2, 3.0, ((0, 4), (1, 128)), jnp.float32),
        "position": jnp.clip(jax.random.uniform(seeds[1], (3, PER_LEAF, LEAVES), jnp.float32, -1.0, 1.0) * shard_levels(seeds[1], (3, PER_LEAF, LEAVES), ((1, 4), (2, 128)), -0.4, 0.0), -1.0, 1.0),
        "charge_count": draw_charge_count(jax.random.fold_in(seeds[10], 71), 0),
        "octant": draw_octant(jax.random.fold_in(seeds[10], 71), 0),
        "shift_ops": normal_values(seeds[4], (8, OPW), (NCOEF * 8) ** -0.5, 0.15625),
        "m2l_ops": normal_values(seeds[5], (NOPS, OPW), (NCOEF * 128) ** -0.5, 0.0390625, ((0, 4),)),
        "let_send": place_ends(jax.random.randint(seeds[6], (N_LEAF, 2 * REACH, CAP), 0, LEAF_DEV), jax.random.fold_in(seeds[6], 1), 0, LEAF_DEV - 1).astype(jnp.int32),
        "list_src": draw_list_src(jax.random.fold_in(seeds[10], 71), 0),
        "list_dst": place_ends(jax.random.randint(seeds[8], (N_LEAF, NOPS, BATCH), 0, LEAF_DEV), jax.random.fold_in(seeds[8], 1), 0, LEAF_DEV - 1).astype(jnp.int32),
        "batch_count": draw_batch_count(jax.random.fold_in(seeds[10], 71), 0),
    }


def coef_tables(degree):
    n_list = []
    m_list = []
    for level in range(degree + 1):
        for mode in range(-level, level + 1):
            n_list.append(level)
            m_list.append(mode)
    n_arr = np.array(n_list, dtype=np.int32)
    m_arr = np.array(m_list, dtype=np.int32)
    return n_arr, np.abs(m_arr), m_arr >= 0


def chebyshev(values, degree):
    terms = [jnp.ones_like(values), values]
    for level in range(2, degree + 1):
        terms.append(2.0 * values * terms[-1] - terms[-2])
    return jnp.stack(terms[:degree + 1], axis=0)


def expand_charges(charges, place, degree):
    slot_count, width = charges.shape
    group = math.gcd(slot_count, 8)
    n_arr, m_abs, use_x = coef_tables(degree)

    def step(index, total):
        block = lax.dynamic_slice_in_dim(charges, index * group, group, 0)
        where = lax.dynamic_slice_in_dim(place, index * group, group, 1)
        cheb_x = chebyshev(where[0], degree)
        cheb_y = chebyshev(where[1], degree)
        cheb_z = chebyshev(where[2], degree)
        basis = cheb_z[n_arr] * jnp.where(use_x[:, None, None], cheb_x[m_abs], cheb_y[m_abs])
        return total + jnp.sum(basis * block[None], axis=1)

    start = jnp.zeros((n_arr.shape[0], width), jnp.float32)
    return lax.fori_loop(0, slot_count // group, step, start)


def unpack_ops(rows, ncoef):
    return rows[:, :ncoef * ncoef].reshape(rows.shape[0], ncoef, ncoef)


def shift_level(columns, octs, shift_mats):
    ncoef, count = columns.shape
    onehot = (octs[:, None] == jnp.arange(8)[None, :]).astype(jnp.float32)
    grouped = columns.astype(jnp.float32).reshape(ncoef, count // 8, 8)
    picked = jnp.einsum('kpc,pco->okp', grouped, onehot.reshape(count // 8, 8, 8))
    parents = jnp.einsum('okj,ojp->kp', shift_mats.astype(jnp.float32), picked)
    return parents.astype(jnp.bfloat16)


def reference(charge, position, charge_count, octant, shift_ops, m2l_ops, let_send, list_src, list_dst, batch_count):
    slot_ids = jnp.arange(PER_LEAF)[:, None]
    masked = jnp.where(slot_ids < charge_count[None, :], charge, 0.0)
    charges_dev = masked.reshape(PER_LEAF, N_LEAF, LEAF_DEV).transpose(1, 0, 2)
    place_dev = position.reshape(3, PER_LEAF, N_LEAF, LEAF_DEV).transpose(2, 0, 1, 3)
    shift_mats = unpack_ops(shift_ops, NCOEF)

    def leaf_expand(pair):
        return expand_charges(pair[0], pair[1], ORDER).astype(jnp.bfloat16)

    leaf_multi = lax.map(leaf_expand, (charges_dev, place_dev))
    octs_dev = octant.reshape(N_LEAF, LEAF_DEV + LEAF_DEV // 8)

    def upward(pair):
        columns, octs = pair
        parents = shift_level(columns, octs[:LEAF_DEV], shift_mats)
        grand = shift_level(parents, octs[LEAF_DEV:], shift_mats)
        return jnp.concatenate([parents, grand], axis=1)

    tree = lax.map(upward, (leaf_multi, octs_dev))
    tree_out = tree.transpose(1, 0, 2).reshape(NCOEF, N_LEAF * TREE_DEV)

    group = math.gcd(OPS_DEV, 8)
    slot = jnp.arange(2 * REACH * CAP, dtype=jnp.int32)
    near_k = slot // CAP
    column = slot % CAP
    offset = jnp.where(near_k < REACH, near_k - REACH, near_k - REACH + 1)

    def translate(device):
        sender = jnp.clip(device + offset, 0, N_LEAF - 1).astype(jnp.int32)
        local_ids = let_send[sender, 2 * REACH - 1 - near_k, column]
        remote = leaf_multi[sender, :, local_ids]
        table = jnp.concatenate([leaf_multi[device], remote.T], axis=1)
        sources = list_src[device]
        targets = list_dst[device]
        live = (jnp.arange(BATCH)[None, :] < batch_count[device][:, None]).astype(jnp.float32)

        def step(index, total):
            op_rows = lax.dynamic_slice_in_dim(m2l_ops, index * group, group, 0)
            operators = unpack_ops(op_rows, NCOEF).astype(jnp.float32)
            src_blk = lax.dynamic_slice_in_dim(sources, index * group, group, 0)
            dst_blk = lax.dynamic_slice_in_dim(targets, index * group, group, 0)
            live_blk = lax.dynamic_slice_in_dim(live, index * group, group, 0)
            gathered = jnp.take(table, src_blk.reshape(-1), axis=1).reshape(NCOEF, group, BATCH).astype(jnp.float32)
            values = jnp.einsum('jkc,cjb->kjb', operators, gathered) * live_blk[None]
            return total.at[:, dst_blk.reshape(-1)].add(values.reshape(NCOEF, group * BATCH))

        start = jnp.zeros((NCOEF, LEAF_DEV), jnp.float32)
        return lax.fori_loop(0, NOPS // group, step, start).astype(jnp.bfloat16)

    locals_dev = lax.map(translate, jnp.arange(N_LEAF, dtype=jnp.int32))
    local_field = locals_dev.transpose(1, 0, 2).reshape(NCOEF, LEAVES)
    return (local_field, tree_out)
```

```python
import functools

import jax
import jax.numpy as jnp
from jax import lax
from jax.experimental import pallas as pl
from jax.experimental.pallas import tpu as pltpu
from jax.sharding import PartitionSpec as P

ORDER = 12
NCOEF = (ORDER + 1) ** 2
ROWS = 176
CHUNK = 48
LEAF = 256
CAP = 128
NEAR = 8
BATCH = 384
OCT = 8
WIDE = 256
HALF = ROWS // 2

MESH = pl.DeviceIdType.MESH
F32 = jnp.float32
BF16 = jnp.bfloat16
NT = (((1,), (1,)), ((), ()))


def iota(shape, dim):
    return lax.broadcasted_iota(jnp.int32, shape, dim)


def onehot(mask):
    return jnp.where(mask, 1.0, 0.0).astype(BF16)


def dot(a, b):
    return jnp.dot(a, b, preferred_element_type=F32)


def dot_nt(a, b):
    return lax.dot_general(a, b, NT, preferred_element_type=F32)


def kernel(
    n_leaf,
    n_list,
    charge,
    position,
    count,
    octant,
    shift_ops,
    m2l_ops,
    let_send,
    list_src,
    list_dst,
    batch_count,
    local_out,
    tree_out,
    tz,
    tx,
    ty,
    acc,
    part,
    rs_buf,
    multi,
    outgoing,
    table,
    flat0,
    flat1,
    m_cat,
    s_cat,
    pick,
    z_cat,
    total,
    fin,
    fin_buf,
    rs_send,
    rs_recv,
    ag_send,
    ag_recv,
    halo_send,
    halo_recv,
    fin_send,
    fin_recv,
):
    n_ops = m2l_ops.shape[0]
    all_ops = n_ops + OCT
    slots = charge.shape[0]
    me_leaf = lax.axis_index("leaf")
    me = lax.axis_index("list")
    offsets = [k - NEAR // 2 if k < NEAR // 2 else k - NEAR // 2 + 1 for k in range(NEAR)]
    near_ids = [lax.rem(me_leaf + off + n_leaf, n_leaf) for off in offsets]
    peers = [lax.rem(me + r, n_list) for r in range(1, n_list)]

    barrier = pltpu.get_barrier_semaphore()
    for near in near_ids:
        pl.semaphore_signal(barrier, inc=1, device_id=(near, me), device_id_type=MESH)
    for peer in peers:
        pl.semaphore_signal(barrier, inc=1, device_id=(me_leaf, peer), device_id_type=MESH)

    slot_ids = me * slots + iota((slots, LEAF), 0)
    q = jnp.where(slot_ids < count[...], charge[...], 0.0)
    for axis, dst in ((0, tx), (1, ty), (2, tz)):
        v = position[axis]
        scale = q if axis == 2 else jnp.ones_like(v)
        prev, cur = scale, v * scale
        dst[0] = prev
        dst[1] = cur
        for n in range(2, ORDER + 1):
            prev, cur = cur, 2.0 * v * cur - prev
            dst[n] = cur
    for lane in range(LEAF // 128):
        cols = slice(lane * 128, lane * 128 + 128)
        acc[lane, NCOEF * 8 :, :] = jnp.zeros((acc.shape[1] - NCOEF * 8, 128), F32)
        for n in range(ORDER + 1):
            zn = tz[n, :, cols]
            for m in range(-n, n + 1):
                c = n * n + n + m
                if m > 0:
                    term = zn * tx[m, :, cols]
                elif m < 0:
                    term = zn * ty[-m, :, cols]
                else:
                    term = zn
                acc[lane, c * 8 : c * 8 + 8, :] = jnp.sum(term.reshape(slots // 8, 8, 128), axis=0)
        for chunk in range(n_list):
            s = acc[lane, pl.ds(chunk * CHUNK * 8, CHUNK, stride=8), :]
            for i in range(1, 8):
                s = s + acc[lane, pl.ds(chunk * CHUNK * 8 + i, CHUNK, stride=8), :]
            part[chunk, :, cols] = s

    pl.semaphore_wait(barrier, NEAR + n_list - 1)

    rs = []
    for r in range(1, n_list):
        copy = pltpu.make_async_remote_copy(
            src_ref=part.at[peers[r - 1]],
            dst_ref=rs_buf.at[r - 1],
            send_sem=rs_send.at[r - 1],
            recv_sem=rs_recv.at[r - 1],
            device_id=(me_leaf, peers[r - 1]),
            device_id_type=MESH,
        )
        copy.start()
        rs.append(copy)

    tail = pl.ds(NCOEF * all_ops, (ROWS - NCOEF) * all_ops)
    flat0[tail, :] = jnp.zeros(((ROWS - NCOEF) * all_ops, 128), F32)
    flat1[tail, :] = jnp.zeros(((ROWS - NCOEF) * all_ops, 128), F32)

    def align_row(k, _):
        start = k * NCOEF
        first = start // 128
        turn = start - first * 128
        back = lax.rem(128 - turn, 128)
        for ref, at in ((m2l_ops, 0), (shift_ops, n_ops)):
            count_ops = ref.shape[0]
            lanes = iota((count_ops, 128), 1)
            pieces = [
                pltpu.roll(
                    ref[:, pl.ds(pl.multiple_of((first + i) * 128, 128), 128)].astype(F32), back, 1
                )
                for i in range(3)
            ]
            keep = lanes < 128 - turn
            rows = pl.ds(pl.multiple_of(k * all_ops + at, 8), count_ops)
            flat0[rows, :] = jnp.where(keep, pieces[0], pieces[1])
            flat1[rows, :] = jnp.where(
                lanes < NCOEF - 128, jnp.where(keep, pieces[1], pieces[2]), 0.0
            )
        return 0

    lax.fori_loop(0, NCOEF, align_row, 0)

    for copy in rs:
        copy.wait()
    mine = part[me]
    for r in range(1, n_list):
        mine = mine + rs_buf[r - 1]
    multi[me] = mine.astype(BF16)
    ag = []
    for r in range(1, n_list):
        copy = pltpu.make_async_remote_copy(
            src_ref=multi.at[me],
            dst_ref=multi.at[me],
            send_sem=ag_send.at[r - 1],
            recv_sem=ag_recv.at[r - 1],
            device_id=(me_leaf, peers[r - 1]),
            device_id_type=MESH,
        )
        copy.start()
        ag.append(copy)

    def take_op(g, _):
        cols = pl.multiple_of(g * WIDE, WIDE)
        m_cat[:, pl.ds(cols, 128)] = flat0[pl.ds(g, ROWS, stride=all_ops), :].astype(BF16)
        m_cat[:, pl.ds(cols + 128, 128)] = flat1[pl.ds(g, ROWS, stride=all_ops), :].astype(BF16)
        return 0

    lax.fori_loop(0, n_ops, take_op, 0)
    for o in range(OCT):
        rows = pl.ds(n_ops + o, ROWS, stride=all_ops)
        s_cat[:, o * WIDE : o * WIDE + 128] = flat0[rows, :].astype(BF16)
        s_cat[:, o * WIDE + 128 : o * WIDE + 256] = flat1[rows, :].astype(BF16)

    for copy in ag:
        copy.wait()
    leaves = multi[...].reshape(n_list * CHUNK, LEAF)[:ROWS]
    table[:, :LEAF] = leaves

    halo = []
    for k in (0, 7, 1, 6, 2, 5, 3, 4):
        pickers = onehot(iota((LEAF, CAP), 0) == let_send[k : k + 1, :])
        outgoing[k] = dot(leaves, pickers).astype(BF16)
        to = LEAF + (NEAR - 1 - k) * CAP
        copy = pltpu.make_async_remote_copy(
            src_ref=outgoing.at[k],
            dst_ref=table.at[:, to : to + CAP],
            send_sem=halo_send.at[k],
            recv_sem=halo_recv.at[k],
            device_id=(near_ids[k], me),
            device_id_type=MESH,
        )
        copy.start()
        halo.append(copy)

    pick[...] = jnp.zeros_like(pick)
    child = iota((128, LEAF), 1)
    cell = iota((128, LEAF), 0)
    octs = octant[0:1, 0:LEAF]
    for o in range(OCT):
        chosen = onehot(cell == jnp.where(octs == o, child // 8, -1))
        pick[o * WIDE : o * WIDE + ROWS, :] = dot_nt(leaves, chosen).astype(BF16)
    parents = dot(s_cat[...], pick[...]).astype(BF16)
    n_par = LEAF // 8
    child = iota((128, n_par), 1)
    cell = iota((128, n_par), 0)
    octs = octant[0:1, LEAF : LEAF + n_par]
    for o in range(OCT):
        chosen = onehot(cell == jnp.where(octs == o, n_par + child // 8, -1))
        pick[o * WIDE : o * WIDE + ROWS, :] = dot_nt(parents[:, :n_par], chosen).astype(BF16)
    grand = dot(s_cat[...], pick[...])
    tree = jnp.where(iota((ROWS, 128), 1) < n_par, parents.astype(F32), grand).astype(BF16)
    tree_out[...] = tree[:NCOEF, : n_par + n_par // 8]

    for copy in halo:
        copy.wait()

    def gather_op(g, _):
        src = list_src[pl.ds(g, 1), :]
        dst = list_dst[pl.ds(g, 1), :]
        src = jnp.where(iota((1, BATCH), 1) < batch_count[0, g], src, -1)
        x = jnp.zeros((ROWS, BATCH), F32)
        for h in range(table.shape[1] // 256):
            hot = onehot(iota((256, BATCH), 0) + h * 256 == src)
            x = x + dot(table[:, h * 256 : h * 256 + 256], hot)
        hot = onehot(iota((LEAF, BATCH), 0) == dst)
        z = dot_nt(x.astype(BF16), hot).astype(BF16)
        z_cat[pl.ds(pl.multiple_of(g * WIDE, WIDE), ROWS), :] = z
        z_cat[pl.ds(pl.multiple_of(g * WIDE + ROWS, 16), WIDE - ROWS), :] = jnp.zeros(
            (WIDE - ROWS, LEAF), BF16
        )
        return 0

    lax.fori_loop(0, n_ops, gather_op, 0)
    total[...] = dot(m_cat[...], z_cat[...])

    left = iota((HALF, 128), 1) < 64
    for j in range(n_list):
        cols = slice(j // 2 * 128, j // 2 * 128 + 128)
        top, low = total[:HALF, cols], total[HALF:, cols]
        if j % 2 == 0:
            fin[j] = jnp.where(left, top, pltpu.roll(low, 64, 1))
        else:
            fin[j] = jnp.where(left, pltpu.roll(top, 64, 1), low)
    last = []
    for r in range(1, n_list):
        copy = pltpu.make_async_remote_copy(
            src_ref=fin.at[peers[r - 1]],
            dst_ref=fin_buf.at[r - 1],
            send_sem=fin_send.at[r - 1],
            recv_sem=fin_recv.at[r - 1],
            device_id=(me_leaf, peers[r - 1]),
            device_id_type=MESH,
        )
        copy.start()
        last.append(copy)
    for copy in last:
        copy.wait()
    s = fin[me]
    for r in range(1, n_list):
        s = s + fin_buf[r - 1]
    local_out[:HALF, :] = s[:, :64].astype(BF16)
    local_out[HALF:, :] = pltpu.roll(s, 64, 1)[: NCOEF - HALF, :64].astype(BF16)


def per_device(
    n_leaf,
    n_list,
    charge,
    position,
    charge_count,
    octant,
    shift_ops,
    m2l_ops,
    let_send,
    list_src,
    list_dst,
    batch_count,
):
    slots = charge.shape[0]
    n_ops = m2l_ops.shape[0]
    all_ops = n_ops + OCT
    columns = LEAF + NEAR * CAP
    vmem = pl.BlockSpec(memory_space=pltpu.VMEM)
    dma = pltpu.SemaphoreType.DMA
    return pl.pallas_call(
        functools.partial(kernel, n_leaf, n_list),
        out_shape=(
            jax.ShapeDtypeStruct((NCOEF, LEAF // n_list), BF16),
            jax.ShapeDtypeStruct((NCOEF, LEAF // 8 + LEAF // 64), BF16),
        ),
        in_specs=[vmem] * 9 + [pl.BlockSpec(memory_space=pltpu.SMEM)],
        out_specs=(vmem, vmem),
        scratch_shapes=[
            pltpu.VMEM((ORDER + 1, slots, LEAF), F32),
            pltpu.VMEM((ORDER + 1, slots, LEAF), F32),
            pltpu.VMEM((ORDER + 1, slots, LEAF), F32),
            pltpu.VMEM((LEAF // 128, n_list * CHUNK * 8, 128), F32),
            pltpu.VMEM((n_list, CHUNK, LEAF), F32),
            pltpu.VMEM((n_list - 1, CHUNK, LEAF), F32),
            pltpu.VMEM((n_list, CHUNK, LEAF), BF16),
            pltpu.VMEM((NEAR, ROWS, CAP), BF16),
            pltpu.VMEM((ROWS, columns), BF16),
            pltpu.VMEM((ROWS * all_ops, 128), F32),
            pltpu.VMEM((ROWS * all_ops, 128), F32),
            pltpu.VMEM((ROWS, n_ops * WIDE), BF16),
            pltpu.VMEM((ROWS, OCT * WIDE), BF16),
            pltpu.VMEM((OCT * WIDE, 128), BF16),
            pltpu.VMEM((n_ops * WIDE, LEAF), BF16),
            pltpu.VMEM((ROWS, LEAF), F32),
            pltpu.VMEM((n_list, HALF, 128), F32),
            pltpu.VMEM((n_list - 1, HALF, 128), F32),
            dma((n_list - 1,)),
            dma((n_list - 1,)),
            dma((n_list - 1,)),
            dma((n_list - 1,)),
            dma((NEAR,)),
            dma((NEAR,)),
            dma((n_list - 1,)),
            dma((n_list - 1,)),
        ],
        compiler_params=pltpu.CompilerParams(
            collective_id=0, has_side_effects=True, vmem_limit_bytes=56 << 20
        ),
    )(
        charge,
        position,
        charge_count.reshape(1, -1),
        octant.reshape(1, -1),
        shift_ops,
        m2l_ops,
        let_send[0],
        list_src[0],
        list_dst[0],
        batch_count,
    )


def solution(mesh):
    return jax.shard_map(
        functools.partial(per_device, mesh.shape["leaf"], mesh.shape["list"]),
        mesh=mesh,
        in_specs=(
            P("list", "leaf"),
            P(None, "list", "leaf"),
            P("leaf"),
            P("leaf"),
            P(),
            P("list", None),
            P("leaf", None, None),
            P("leaf", "list", None),
            P("leaf", "list", None),
            P("leaf", "list"),
        ),
        out_specs=(P(None, ("leaf", "list")), P(None, "leaf")),
        check_vma=False,
    )
```

```python
import functools

import jax
import jax.numpy as jnp
from jax import lax
from jax.experimental import pallas as pl
from jax.experimental.pallas import tpu as pltpu
from jax.sharding import PartitionSpec as P

ORDER = 12
NCOEF = (ORDER + 1) ** 2
ROWS = 176
CHUNK = 48
LEAF = 256
CAP = 128
NEAR = 8
BATCH = 384
OCT = 8
WIDE = 256
HALF = ROWS // 2
BLOCK = 4
IN_PARTS = 4
SPREAD = 56

MESH = pl.DeviceIdType.MESH
F32 = jnp.float32
BF16 = jnp.bfloat16
NT = (((1,), (1,)), ((), ()))


def iota(shape, dim):
    return lax.broadcasted_iota(jnp.int32, shape, dim)


def onehot(mask):
    return jnp.where(mask, 1.0, 0.0).astype(BF16)


def dot(a, b):
    return jnp.dot(a, b, preferred_element_type=F32)


def dot_nt(a, b):
    return lax.dot_general(a, b, NT, preferred_element_type=F32)


def kernel(
    n_leaf,
    n_list,
    charge_hbm,
    position_hbm,
    count,
    octant,
    shift_hbm,
    m2l_hbm,
    let_send,
    src_hbm,
    dst_hbm,
    batch_count,
    local_out,
    tree_out,
    charge,
    position,
    shift_ops,
    m2l_ops,
    list_src,
    list_dst,
    tz,
    tx,
    ty,
    acc,
    part,
    rs_buf,
    multi,
    outgoing,
    table,
    flat0,
    flat1,
    m_cat,
    s_cat,
    pick,
    x_buf,
    z_buf,
    total,
    fin,
    fin_buf,
    rs_send,
    rs_recv,
    ag_send,
    ag_recv,
    halo_send,
    halo_recv,
    fin_send,
    fin_recv,
    in_sem,
):
    n_ops = m2l_ops.shape[0]
    all_ops = SPREAD
    slots = charge.shape[0]
    me_leaf = lax.axis_index("leaf")
    me = lax.axis_index("list")
    offsets = [k - NEAR // 2 if k < NEAR // 2 else k - NEAR // 2 + 1 for k in range(NEAR)]
    near_ids = [lax.rem(me_leaf + off + n_leaf, n_leaf) for off in offsets]
    peers = [lax.rem(me + r, n_list) for r in range(1, n_list)]

    charges_in = [
        pltpu.make_async_copy(charge_hbm, charge, in_sem.at[0]),
        pltpu.make_async_copy(position_hbm, position, in_sem.at[1]),
    ]
    step = m2l_ops.shape[1] // IN_PARTS
    ops_in = [
        pltpu.make_async_copy(
            m2l_hbm.at[:, i * step : i * step + step],
            m2l_ops.at[:, i * step : i * step + step],
            in_sem.at[5 + i],
        )
        for i in range(IN_PARTS)
    ]
    lists_in = [
        pltpu.make_async_copy(src_hbm, list_src, in_sem.at[3]),
        pltpu.make_async_copy(dst_hbm, list_dst, in_sem.at[4]),
    ]
    ops_in.append(pltpu.make_async_copy(shift_hbm, shift_ops, in_sem.at[2]))
    for copy in charges_in + ops_in + lists_in:
        copy.start()

    barrier = pltpu.get_barrier_semaphore()
    for near in near_ids:
        pl.semaphore_signal(barrier, inc=1, device_id=(near, me), device_id_type=MESH)
    for peer in peers:
        pl.semaphore_signal(barrier, inc=1, device_id=(me_leaf, peer), device_id_type=MESH)

    for copy in charges_in:
        copy.wait()
    slot_ids = me * slots + iota((slots, LEAF), 0)
    q = jnp.where(slot_ids < count[...], charge[...], 0.0)
    for axis, dst in ((0, tx), (1, ty), (2, tz)):
        v = position[axis]
        scale = q if axis == 2 else jnp.ones_like(v)
        prev, cur = scale, v * scale
        dst[0] = prev
        dst[1] = cur
        for n in range(2, ORDER + 1):
            prev, cur = cur, 2.0 * v * cur - prev
            dst[n] = cur
    for lane in range(LEAF // 128):
        cols = slice(lane * 128, lane * 128 + 128)
        acc[lane, NCOEF * 8 :, :] = jnp.zeros((acc.shape[1] - NCOEF * 8, 128), F32)
        for n in range(ORDER + 1):
            zn = tz[n, :, cols]
            for m in range(-n, n + 1):
                c = n * n + n + m
                if m > 0:
                    term = zn * tx[m, :, cols]
                elif m < 0:
                    term = zn * ty[-m, :, cols]
                else:
                    term = zn
                acc[lane, c * 8 : c * 8 + 8, :] = jnp.sum(term.reshape(slots // 8, 8, 128), axis=0)
        for chunk in range(n_list):
            s = acc[lane, pl.ds(chunk * CHUNK * 8, CHUNK, stride=8), :]
            for i in range(1, 8):
                s = s + acc[lane, pl.ds(chunk * CHUNK * 8 + i, CHUNK, stride=8), :]
            part[chunk, :, cols] = s

    pl.semaphore_wait(barrier, NEAR + n_list - 1)

    rs = []
    for r in range(1, n_list):
        copy = pltpu.make_async_remote_copy(
            src_ref=part.at[peers[r - 1]],
            dst_ref=rs_buf.at[r - 1],
            send_sem=rs_send.at[r - 1],
            recv_sem=rs_recv.at[r - 1],
            device_id=(me_leaf, peers[r - 1]),
            device_id_type=MESH,
        )
        copy.start()
        rs.append(copy)

    tail = pl.ds(NCOEF * all_ops, (ROWS - NCOEF) * all_ops)
    flat0[tail, :] = jnp.zeros(((ROWS - NCOEF) * all_ops, 128), F32)
    flat1[tail, :] = jnp.zeros(((ROWS - NCOEF) * all_ops, 128), F32)

    def align_row(k, _):
        start = k * NCOEF
        first = start // 128
        turn = start - first * 128
        back = lax.rem(128 - turn, 128)
        for ref, at in ((m2l_ops, 0), (shift_ops, n_ops)):
            count_ops = ref.shape[0]
            lanes = iota((count_ops, 128), 1)
            pieces = [
                pltpu.roll(
                    ref[:, pl.ds(pl.multiple_of((first + i) * 128, 128), 128)].astype(F32), back, 1
                )
                for i in range(3)
            ]
            keep = lanes < 128 - turn
            rows = pl.ds(pl.multiple_of(k * all_ops + at, 8), count_ops)
            flat0[rows, :] = jnp.where(keep, pieces[0], pieces[1])
            flat1[rows, :] = jnp.where(
                lanes < NCOEF - 128, jnp.where(keep, pieces[1], pieces[2]), 0.0
            )
        return 0

    for copy in ops_in:
        copy.wait()
    lax.fori_loop(0, 91, align_row, 0, unroll=13)

    for copy in rs:
        copy.wait()
    mine = part[me]
    for r in range(1, n_list):
        mine = mine + rs_buf[r - 1]
    multi[me] = mine.astype(BF16)
    ag = []
    for r in range(1, n_list):
        copy = pltpu.make_async_remote_copy(
            src_ref=multi.at[me],
            dst_ref=multi.at[me],
            send_sem=ag_send.at[r - 1],
            recv_sem=ag_recv.at[r - 1],
            device_id=(me_leaf, peers[r - 1]),
            device_id_type=MESH,
        )
        copy.start()
        ag.append(copy)

    lax.fori_loop(91, NCOEF, align_row, 0, unroll=13)

    for copy in ag:
        copy.wait()
    leaves = multi[...].reshape(n_list * CHUNK, LEAF)[:ROWS]
    table[:, :LEAF] = leaves

    halo = []
    for k in (0, 7, 1, 6, 2, 5, 3, 4):
        pickers = onehot(iota((LEAF, CAP), 0) == let_send[k : k + 1, :])
        outgoing[k] = dot(leaves, pickers).astype(BF16)
        to = LEAF + (NEAR - 1 - k) * CAP
        copy = pltpu.make_async_remote_copy(
            src_ref=outgoing.at[k],
            dst_ref=table.at[:, to : to + CAP],
            send_sem=halo_send.at[k],
            recv_sem=halo_recv.at[k],
            device_id=(near_ids[k], me),
            device_id_type=MESH,
        )
        copy.start()
        halo.append(copy)

    def take_op(g, _):
        cols = pl.multiple_of(g * WIDE, WIDE)
        m_cat[:, pl.ds(cols, 128)] = flat0[pl.ds(g, ROWS, stride=all_ops), :].astype(BF16)
        m_cat[:, pl.ds(cols + 128, 128)] = flat1[pl.ds(g, ROWS, stride=all_ops), :].astype(BF16)
        return 0

    lax.fori_loop(0, n_ops, take_op, 0, unroll=4)
    for o in range(OCT):
        rows = pl.ds(n_ops + o, ROWS, stride=all_ops)
        s_cat[:, o * WIDE : o * WIDE + 128] = flat0[rows, :].astype(BF16)
        s_cat[:, o * WIDE + 128 : o * WIDE + 256] = flat1[rows, :].astype(BF16)

    pick[...] = jnp.zeros_like(pick)
    child = iota((128, LEAF), 1)
    cell = iota((128, LEAF), 0)
    octs = octant[pl.ds(0, LEAF)].reshape(1, LEAF)
    for o in range(OCT):
        chosen = onehot(cell == jnp.where(octs == o, child // 8, -1))
        pick[o * WIDE : o * WIDE + ROWS, :] = dot_nt(leaves, chosen).astype(BF16)
    parents = dot(s_cat[...], pick[...]).astype(BF16)
    n_par = LEAF // 8
    child = iota((128, n_par), 1)
    cell = iota((128, n_par), 0)
    octs = octant[pl.ds(LEAF, n_par)].reshape(1, n_par)
    for o in range(OCT):
        chosen = onehot(cell == jnp.where(octs == o, n_par + child // 8, -1))
        pick[o * WIDE : o * WIDE + ROWS, :] = dot_nt(parents[:, :n_par], chosen).astype(BF16)
    grand = dot(s_cat[...], pick[...])
    tree = jnp.where(iota((ROWS, 128), 1) < n_par, parents.astype(F32), grand)
    tree_out[...] = tree.T[: n_par + n_par // 8, :NCOEF].astype(BF16)

    for copy in halo:
        copy.wait()

    for copy in lists_in:
        copy.wait()

    def hot16(row, base, n):
        ids = iota((n, row.shape[1]), 0).astype(jnp.int16)
        return jnp.where(ids == (row - base).astype(jnp.int16), jnp.array(1, BF16), jnp.array(0, BF16))

    def gather(i):
        for u in range(BLOCK):
            g = i * BLOCK + u
            src = list_src[pl.ds(g, 1), :]
            src = jnp.where(iota((1, BATCH), 1) < batch_count[0, g], src, -1)
            x = jnp.zeros((ROWS, BATCH), F32)
            for h in range(table.shape[1] // 256):
                x = x + dot(table[:, h * 256 : h * 256 + 256], hot16(src, h * 256, 256))
            x_buf[lax.rem(i, 2), u] = x.astype(BF16)

    def scatter(i):
        for u in range(BLOCK):
            dst = list_dst[pl.ds(i * BLOCK + u, 1), :]
            z = dot_nt(x_buf[lax.rem(i, 2), u], hot16(dst, 0, LEAF))
            z_buf[lax.rem(i, 2), u * WIDE : u * WIDE + ROWS, :] = z.astype(BF16)

    def apply(i):
        cols = pl.ds(pl.multiple_of(i * (BLOCK * WIDE), BLOCK * WIDE), BLOCK * WIDE)
        total[...] += dot(m_cat[:, cols], z_buf[lax.rem(i, 2)])

    blocks = n_ops // BLOCK
    total[...] = jnp.zeros_like(total)
    z_buf[...] = jnp.zeros_like(z_buf)
    gather(jnp.int32(0))
    scatter(jnp.int32(0))
    gather(jnp.int32(1))

    def steps(i, _):
        apply(i - 2)
        scatter(i - 1)
        gather(i)
        return 0

    lax.fori_loop(2, blocks, steps, 0)
    apply(jnp.int32(blocks - 2))
    scatter(jnp.int32(blocks - 1))
    apply(jnp.int32(blocks - 1))

    left = iota((HALF, 128), 1) < 64
    for j in range(n_list):
        cols = slice(j // 2 * 128, j // 2 * 128 + 128)
        top, low = total[:HALF, cols], total[HALF:, cols]
        if j % 2 == 0:
            fin[j] = jnp.where(left, top, pltpu.roll(low, 64, 1))
        else:
            fin[j] = jnp.where(left, pltpu.roll(top, 64, 1), low)
    last = []
    for r in range(1, n_list):
        copy = pltpu.make_async_remote_copy(
            src_ref=fin.at[peers[r - 1]],
            dst_ref=fin_buf.at[r - 1],
            send_sem=fin_send.at[r - 1],
            recv_sem=fin_recv.at[r - 1],
            device_id=(me_leaf, peers[r - 1]),
            device_id_type=MESH,
        )
        copy.start()
        last.append(copy)
    for copy in last:
        copy.wait()
    s = fin[me]
    for r in range(1, n_list):
        s = s + fin_buf[r - 1]
    s = jnp.concatenate([s, pltpu.roll(s, 64, 1)], axis=0)
    local_out[...] = s.T[:64, :NCOEF].astype(BF16)


def per_device(
    n_leaf,
    n_list,
    charge,
    position,
    charge_count,
    octant,
    shift_ops,
    m2l_ops,
    let_send,
    list_src,
    list_dst,
    batch_count,
):
    slots = charge.shape[0]
    n_ops = m2l_ops.shape[0]
    all_ops = SPREAD
    columns = LEAF + NEAR * CAP
    vmem = pl.BlockSpec(memory_space=pltpu.VMEM)
    dma = pltpu.SemaphoreType.DMA
    hbm = pl.BlockSpec(memory_space=pl.ANY)
    local_t, tree_t = pl.pallas_call(
        functools.partial(kernel, n_leaf, n_list),
        out_shape=(
            jax.ShapeDtypeStruct((LEAF // n_list, NCOEF), BF16),
            jax.ShapeDtypeStruct((LEAF // 8 + LEAF // 64, NCOEF), BF16),
        ),
        in_specs=[hbm, hbm, vmem, vmem, hbm, hbm, vmem, hbm, hbm, pl.BlockSpec(memory_space=pltpu.SMEM)],
        out_specs=(vmem, vmem),
        scratch_shapes=[
            pltpu.VMEM(charge.shape, F32),
            pltpu.VMEM(position.shape, F32),
            pltpu.VMEM(shift_ops.shape, BF16),
            pltpu.VMEM(m2l_ops.shape, BF16),
            pltpu.VMEM(list_src.shape[1:], jnp.int32),
            pltpu.VMEM(list_src.shape[1:], jnp.int32),
            pltpu.VMEM((ORDER + 1, slots, LEAF), F32),
            pltpu.VMEM((ORDER + 1, slots, LEAF), F32),
            pltpu.VMEM((ORDER + 1, slots, LEAF), F32),
            pltpu.VMEM((LEAF // 128, n_list * CHUNK * 8, 128), F32),
            pltpu.VMEM((n_list, CHUNK, LEAF), F32),
            pltpu.VMEM((n_list - 1, CHUNK, LEAF), F32),
            pltpu.VMEM((n_list, CHUNK, LEAF), BF16),
            pltpu.VMEM((NEAR, ROWS, CAP), BF16),
            pltpu.VMEM((ROWS, columns), BF16),
            pltpu.VMEM((ROWS * all_ops, 128), F32),
            pltpu.VMEM((ROWS * all_ops, 128), F32),
            pltpu.VMEM((ROWS, n_ops * WIDE), BF16),
            pltpu.VMEM((ROWS, OCT * WIDE), BF16),
            pltpu.VMEM((OCT * WIDE, 128), BF16),
            pltpu.VMEM((2, BLOCK, ROWS, BATCH), BF16),
            pltpu.VMEM((2, BLOCK * WIDE, LEAF), BF16),
            pltpu.VMEM((ROWS, LEAF), F32),
            pltpu.VMEM((n_list, HALF, 128), F32),
            pltpu.VMEM((n_list - 1, HALF, 128), F32),
            dma((n_list - 1,)),
            dma((n_list - 1,)),
            dma((n_list - 1,)),
            dma((n_list - 1,)),
            dma((NEAR,)),
            dma((NEAR,)),
            dma((n_list - 1,)),
            dma((n_list - 1,)),
            dma((5 + IN_PARTS,)),
        ],
        compiler_params=pltpu.CompilerParams(
            collective_id=0, has_side_effects=True, vmem_limit_bytes=56 << 20
        ),
    )(
        charge,
        position,
        charge_count.reshape(1, -1),
        octant,
        shift_ops,
        m2l_ops,
        let_send[0],
        list_src[0],
        list_dst[0],
        batch_count,
    )
    return local_t.T, tree_t.T


def solution(mesh):
    return jax.shard_map(
        functools.partial(per_device, mesh.shape["leaf"], mesh.shape["list"]),
        mesh=mesh,
        in_specs=(
            P("list", "leaf"),
            P(None, "list", "leaf"),
            P("leaf"),
            P("leaf"),
            P(),
            P("list", None),
            P("leaf", None, None),
            P("leaf", "list", None),
            P("leaf", "list", None),
            P("leaf", "list"),
        ),
        out_specs=(P(None, ("leaf", "list")), P(None, "leaf")),
        check_vma=False,
    )
```

```python
import functools

import jax
import jax.numpy as jnp
from jax import lax
from jax.experimental import pallas as pl
from jax.experimental.pallas import tpu as pltpu
from jax.sharding import PartitionSpec as P

ORDER = 12
NCOEF = (ORDER + 1) ** 2
ROWS = 176
CHUNK = 48
LEAF = 256
CAP = 128
NEAR = 8
BATCH = 384
OCT = 8
WIDE = 256
HALF = ROWS // 2
BLOCK = 8
IN_PARTS = 4
TILES = 1 + NEAR * CAP // LEAF
PAIR = 2
SPREAD = 56

MESH = pl.DeviceIdType.MESH
F32 = jnp.float32
BF16 = jnp.bfloat16
NT = (((1,), (1,)), ((), ()))


def iota(shape, dim):
    return lax.broadcasted_iota(jnp.int32, shape, dim)


def onehot(mask):
    return jnp.where(mask, 1.0, 0.0).astype(BF16)


def dot(a, b):
    return jnp.dot(a, b, preferred_element_type=F32)


def dot_nt(a, b):
    return lax.dot_general(a, b, NT, preferred_element_type=F32)


def kernel(
    n_leaf,
    n_list,
    charge_hbm,
    position_hbm,
    count,
    octant,
    shift_hbm,
    m2l_hbm,
    let_send,
    src_hbm,
    dst_hbm,
    batch_count,
    local_out,
    tree_out,
    charge,
    position,
    shift_ops,
    m2l_ops,
    list_src,
    list_dst,
    tz,
    tx,
    ty,
    acc,
    part,
    rs_buf,
    multi,
    outgoing,
    table,
    flat0,
    flat1,
    m_cat,
    s_cat,
    pick,
    x_own,
    x_buf,
    z_buf,
    total,
    fin,
    fin_buf,
    rs_send,
    rs_recv,
    ag_send,
    ag_recv,
    halo_send,
    halo_recv,
    fin_send,
    fin_recv,
    in_sem,
):
    n_ops = m2l_ops.shape[0]
    all_ops = SPREAD
    slots = charge.shape[0]
    me_leaf = lax.axis_index("leaf")
    me = lax.axis_index("list")
    offsets = [k - NEAR // 2 if k < NEAR // 2 else k - NEAR // 2 + 1 for k in range(NEAR)]
    near_ids = [lax.rem(me_leaf + off + n_leaf, n_leaf) for off in offsets]
    peers = [lax.rem(me + r, n_list) for r in range(1, n_list)]

    charges_in = [
        pltpu.make_async_copy(charge_hbm, charge, in_sem.at[0]),
        pltpu.make_async_copy(position_hbm, position, in_sem.at[1]),
    ]
    step = m2l_ops.shape[1] // IN_PARTS
    ops_in = [
        pltpu.make_async_copy(
            m2l_hbm.at[:, i * step : i * step + step],
            m2l_ops.at[:, i * step : i * step + step],
            in_sem.at[5 + i],
        )
        for i in range(IN_PARTS)
    ]
    lists_in = [
        pltpu.make_async_copy(src_hbm, list_src, in_sem.at[3]),
        pltpu.make_async_copy(dst_hbm, list_dst, in_sem.at[4]),
    ]
    ops_in.append(pltpu.make_async_copy(shift_hbm, shift_ops, in_sem.at[2]))
    for copy in charges_in + ops_in + lists_in:
        copy.start()

    barrier = pltpu.get_barrier_semaphore()
    for near in near_ids:
        pl.semaphore_signal(barrier, inc=1, device_id=(near, me), device_id_type=MESH)
    for peer in peers:
        pl.semaphore_signal(barrier, inc=1, device_id=(me_leaf, peer), device_id_type=MESH)

    for copy in charges_in:
        copy.wait()
    slot_ids = me * slots + iota((slots, LEAF), 0)
    q = jnp.where(slot_ids < count[...], charge[...], 0.0)
    for axis, dst in ((0, tx), (1, ty), (2, tz)):
        v = position[axis]
        scale = q if axis == 2 else jnp.ones_like(v)
        prev, cur = scale, v * scale
        dst[0] = prev
        dst[1] = cur
        for n in range(2, ORDER + 1):
            prev, cur = cur, 2.0 * v * cur - prev
            dst[n] = cur
    for lane in range(LEAF // 128):
        cols = slice(lane * 128, lane * 128 + 128)
        acc[lane, NCOEF * 8 :, :] = jnp.zeros((acc.shape[1] - NCOEF * 8, 128), F32)
        for n in range(ORDER + 1):
            zn = tz[n, :, cols]
            for m in range(-n, n + 1):
                c = n * n + n + m
                if m > 0:
                    term = zn * tx[m, :, cols]
                elif m < 0:
                    term = zn * ty[-m, :, cols]
                else:
                    term = zn
                acc[lane, c * 8 : c * 8 + 8, :] = jnp.sum(term.reshape(slots // 8, 8, 128), axis=0)
        for chunk in range(n_list):
            s = acc[lane, pl.ds(chunk * CHUNK * 8, CHUNK, stride=8), :]
            for i in range(1, 8):
                s = s + acc[lane, pl.ds(chunk * CHUNK * 8 + i, CHUNK, stride=8), :]
            part[chunk, :, cols] = s

    pl.semaphore_wait(barrier, NEAR + n_list - 1)

    rs = []
    for r in range(1, n_list):
        copy = pltpu.make_async_remote_copy(
            src_ref=part.at[peers[r - 1]],
            dst_ref=rs_buf.at[r - 1],
            send_sem=rs_send.at[r - 1],
            recv_sem=rs_recv.at[r - 1],
            device_id=(me_leaf, peers[r - 1]),
            device_id_type=MESH,
        )
        copy.start()
        rs.append(copy)

    tail = pl.ds(NCOEF * all_ops, (ROWS - NCOEF) * all_ops)
    flat0[tail, :] = jnp.zeros(((ROWS - NCOEF) * all_ops, 128), F32)
    flat1[tail, :] = jnp.zeros(((ROWS - NCOEF) * all_ops, 128), F32)

    def align_row(k, _):
        start = k * NCOEF
        first = start // 128
        turn = start - first * 128
        back = lax.rem(128 - turn, 128)
        for ref, at in ((m2l_ops, 0), (shift_ops, n_ops)):
            count_ops = ref.shape[0]
            lanes = iota((count_ops, 128), 1)
            pieces = [
                pltpu.roll(
                    ref[:, pl.ds(pl.multiple_of((first + i) * 128, 128), 128)].astype(F32), back, 1
                )
                for i in range(3)
            ]
            keep = lanes < 128 - turn
            rows = pl.ds(pl.multiple_of(k * all_ops + at, 8), count_ops)
            flat0[rows, :] = jnp.where(keep, pieces[0], pieces[1])
            flat1[rows, :] = jnp.where(
                lanes < NCOEF - 128, jnp.where(keep, pieces[1], pieces[2]), 0.0
            )
        return 0

    for copy in ops_in:
        copy.wait()
    lax.fori_loop(0, 91, align_row, 0, unroll=13)

    for copy in rs:
        copy.wait()
    mine = part[me]
    for r in range(1, n_list):
        mine = mine + rs_buf[r - 1]
    multi[me] = mine.astype(BF16)
    ag = []
    for r in range(1, n_list):
        copy = pltpu.make_async_remote_copy(
            src_ref=multi.at[me],
            dst_ref=multi.at[me],
            send_sem=ag_send.at[r - 1],
            recv_sem=ag_recv.at[r - 1],
            device_id=(me_leaf, peers[r - 1]),
            device_id_type=MESH,
        )
        copy.start()
        ag.append(copy)

    lax.fori_loop(91, NCOEF, align_row, 0, unroll=13)

    for copy in ag:
        copy.wait()
    leaves = multi[...].reshape(n_list * CHUNK, LEAF)[:ROWS]
    table[0] = leaves

    halo = []
    for k in (0, 7, 1, 6, 2, 5, 3, 4):
        pickers = onehot(iota((LEAF, CAP), 0) == let_send[k : k + 1, :])
        outgoing[k] = dot(leaves, pickers).astype(BF16)
        to = NEAR - 1 - k
        copy = pltpu.make_async_remote_copy(
            src_ref=outgoing.at[k],
            dst_ref=table.at[1 + to // 2, :, to % 2 * CAP : to % 2 * CAP + CAP],
            send_sem=halo_send.at[k],
            recv_sem=halo_recv.at[k],
            device_id=(near_ids[k], me),
            device_id_type=MESH,
        )
        copy.start()
        halo.append(copy)

    def take_op(g, _):
        cols = pl.multiple_of(g * WIDE, WIDE)
        m_cat[:, pl.ds(cols, 128)] = flat0[pl.ds(g, ROWS, stride=all_ops), :].astype(BF16)
        m_cat[:, pl.ds(cols + 128, 128)] = flat1[pl.ds(g, ROWS, stride=all_ops), :].astype(BF16)
        return 0

    lax.fori_loop(0, n_ops, take_op, 0, unroll=4)
    for o in range(OCT):
        rows = pl.ds(n_ops + o, ROWS, stride=all_ops)
        s_cat[:, o * WIDE : o * WIDE + 128] = flat0[rows, :].astype(BF16)
        s_cat[:, o * WIDE + 128 : o * WIDE + 256] = flat1[rows, :].astype(BF16)

    pick[...] = jnp.zeros_like(pick)
    child = iota((128, LEAF), 1)
    cell = iota((128, LEAF), 0)
    octs = octant[pl.ds(0, LEAF)].reshape(1, LEAF)
    for o in range(OCT):
        chosen = onehot(cell == jnp.where(octs == o, child // 8, -1))
        pick[o * WIDE : o * WIDE + ROWS, :] = dot_nt(leaves, chosen).astype(BF16)
    parents = dot(s_cat[...], pick[...]).astype(BF16)
    n_par = LEAF // 8
    child = iota((128, n_par), 1)
    cell = iota((128, n_par), 0)
    octs = octant[pl.ds(LEAF, n_par)].reshape(1, n_par)
    for o in range(OCT):
        chosen = onehot(cell == jnp.where(octs == o, n_par + child // 8, -1))
        pick[o * WIDE : o * WIDE + ROWS, :] = dot_nt(parents[:, :n_par], chosen).astype(BF16)
    grand = dot(s_cat[...], pick[...])
    tree = jnp.where(iota((ROWS, 128), 1) < n_par, parents.astype(F32), grand)
    tree_out[...] = tree


    for copy in lists_in:
        copy.wait()

    def hot16(row, base, n):
        ids = iota((n, row.shape[1]), 0).astype(jnp.int16)
        return jnp.where(ids == (row - base).astype(jnp.int16), jnp.array(1, BF16), jnp.array(0, BF16))

    def sources(g):
        rows = []
        for v in range(PAIR):
            src = list_src[pl.ds(g + v, 1), :]
            rows.append(jnp.where(iota((1, BATCH), 1) < batch_count[0, g + v], src, TILES * LEAF))
        return jnp.concatenate(rows, axis=1)

    def gather_own(p, _):
        x_own[p] = dot(leaves, hot16(sources(p * PAIR), 0, LEAF)).astype(BF16)
        return 0

    lax.fori_loop(0, n_ops // PAIR, gather_own, 0, unroll=4)
    for copy in halo:
        copy.wait()

    def gather(i):
        for u in range(0, BLOCK, PAIR):
            src = sources(i * BLOCK + u)
            tile = src // LEAF
            others = table[1:].reshape((TILES - 1) * ROWS, LEAF)
            each = dot(others, hot16(src - tile * LEAF, 0, LEAF))
            x = x_own[i * (BLOCK // PAIR) + u // PAIR].astype(F32)
            for h in range(1, TILES):
                x = jnp.where(tile == h, each[(h - 1) * ROWS : h * ROWS], x)
            for v in range(PAIR):
                x_buf[lax.rem(i, 2), u + v] = x[:, v * BATCH : v * BATCH + BATCH].astype(BF16)

    def scatter(i):
        for u in range(BLOCK):
            dst = list_dst[pl.ds(i * BLOCK + u, 1), :]
            z = dot_nt(x_buf[lax.rem(i, 2), u], hot16(dst, 0, LEAF))
            z_buf[lax.rem(i, 2), u * WIDE : u * WIDE + ROWS, :] = z.astype(BF16)

    def apply(i):
        cols = pl.ds(pl.multiple_of(i * (BLOCK * WIDE), BLOCK * WIDE), BLOCK * WIDE)
        total[...] += dot(m_cat[:, cols], z_buf[lax.rem(i, 2)])

    blocks = n_ops // BLOCK
    total[...] = jnp.zeros_like(total)
    z_buf[...] = jnp.zeros_like(z_buf)
    gather(jnp.int32(0))
    scatter(jnp.int32(0))
    gather(jnp.int32(1))

    def steps(i, _):
        apply(i - 2)
        scatter(i - 1)
        gather(i)
        return 0

    lax.fori_loop(2, blocks, steps, 0)
    apply(jnp.int32(blocks - 2))
    scatter(jnp.int32(blocks - 1))
    apply(jnp.int32(blocks - 1))

    left = iota((HALF, 128), 1) < 64
    for j in range(n_list):
        cols = slice(j // 2 * 128, j // 2 * 128 + 128)
        top, low = total[:HALF, cols], total[HALF:, cols]
        if j % 2 == 0:
            fin[j] = jnp.where(left, top, pltpu.roll(low, 64, 1))
        else:
            fin[j] = jnp.where(left, pltpu.roll(top, 64, 1), low)
    last = []
    for r in range(1, n_list):
        copy = pltpu.make_async_remote_copy(
            src_ref=fin.at[peers[r - 1]],
            dst_ref=fin_buf.at[r - 1],
            send_sem=fin_send.at[r - 1],
            recv_sem=fin_recv.at[r - 1],
            device_id=(me_leaf, peers[r - 1]),
            device_id_type=MESH,
        )
        copy.start()
        last.append(copy)
    for copy in last:
        copy.wait()
    s = fin[me]
    for r in range(1, n_list):
        s = s + fin_buf[r - 1]
    local_out[...] = s


def finish(local, tree, local_out, tree_out):
    s = local[...]
    s = jnp.concatenate([s, pltpu.roll(s, 64, 1)], axis=0)
    local_out[...] = s.T[: local_out.shape[0], :NCOEF].astype(BF16)
    tree_out[...] = tree[...].T[: tree_out.shape[0], :NCOEF].astype(BF16)


def per_device(
    n_leaf,
    n_list,
    charge,
    position,
    charge_count,
    octant,
    shift_ops,
    m2l_ops,
    let_send,
    list_src,
    list_dst,
    batch_count,
):
    slots = charge.shape[0]
    n_ops = m2l_ops.shape[0]
    all_ops = SPREAD
    vmem = pl.BlockSpec(memory_space=pltpu.VMEM)
    dma = pltpu.SemaphoreType.DMA
    hbm = pl.BlockSpec(memory_space=pl.ANY)
    local, tree = pl.pallas_call(
        functools.partial(kernel, n_leaf, n_list),
        out_shape=(
            jax.ShapeDtypeStruct((HALF, 128), F32),
            jax.ShapeDtypeStruct((ROWS, 128), F32),
        ),
        in_specs=[hbm, hbm, vmem, vmem, hbm, hbm, vmem, hbm, hbm, pl.BlockSpec(memory_space=pltpu.SMEM)],
        out_specs=(vmem, vmem),
        scratch_shapes=[
            pltpu.VMEM(charge.shape, F32),
            pltpu.VMEM(position.shape, F32),
            pltpu.VMEM(shift_ops.shape, BF16),
            pltpu.VMEM(m2l_ops.shape, BF16),
            pltpu.VMEM(list_src.shape[1:], jnp.int32),
            pltpu.VMEM(list_src.shape[1:], jnp.int32),
            pltpu.VMEM((ORDER + 1, slots, LEAF), F32),
            pltpu.VMEM((ORDER + 1, slots, LEAF), F32),
            pltpu.VMEM((ORDER + 1, slots, LEAF), F32),
            pltpu.VMEM((LEAF // 128, n_list * CHUNK * 8, 128), F32),
            pltpu.VMEM((n_list, CHUNK, LEAF), F32),
            pltpu.VMEM((n_list - 1, CHUNK, LEAF), F32),
            pltpu.VMEM((n_list, CHUNK, LEAF), BF16),
            pltpu.VMEM((NEAR, ROWS, CAP), BF16),
            pltpu.VMEM((TILES, ROWS, LEAF), BF16),
            pltpu.VMEM((ROWS * all_ops, 128), F32),
            pltpu.VMEM((ROWS * all_ops, 128), F32),
            pltpu.VMEM((ROWS, n_ops * WIDE), BF16),
            pltpu.VMEM((ROWS, OCT * WIDE), BF16),
            pltpu.VMEM((OCT * WIDE, 128), BF16),
            pltpu.VMEM((n_ops // PAIR, ROWS, PAIR * BATCH), BF16),
            pltpu.VMEM((2, BLOCK, ROWS, BATCH), BF16),
            pltpu.VMEM((2, BLOCK * WIDE, LEAF), BF16),
            pltpu.VMEM((ROWS, LEAF), F32),
            pltpu.VMEM((n_list, HALF, 128), F32),
            pltpu.VMEM((n_list - 1, HALF, 128), F32),
            dma((n_list - 1,)),
            dma((n_list - 1,)),
            dma((n_list - 1,)),
            dma((n_list - 1,)),
            dma((NEAR,)),
            dma((NEAR,)),
            dma((n_list - 1,)),
            dma((n_list - 1,)),
            dma((5 + IN_PARTS,)),
        ],
        compiler_params=pltpu.CompilerParams(
            collective_id=0, has_side_effects=True, vmem_limit_bytes=56 << 20
        ),
    )(
        charge,
        position,
        charge_count.reshape(1, -1),
        octant,
        shift_ops,
        m2l_ops,
        let_send[0],
        list_src[0],
        list_dst[0],
        batch_count,
    )
    local_t, tree_t = pl.pallas_call(
        finish,
        out_shape=(
            jax.ShapeDtypeStruct((LEAF // n_list, NCOEF), BF16),
            jax.ShapeDtypeStruct((LEAF // 8 + LEAF // 64, NCOEF), BF16),
        ),
        in_specs=[vmem, vmem],
        out_specs=(vmem, vmem),
    )(local, tree)
    return local_t.T, tree_t.T


def solution(mesh):
    return jax.shard_map(
        functools.partial(per_device, mesh.shape["leaf"], mesh.shape["list"]),
        mesh=mesh,
        in_specs=(
            P("list", "leaf"),
            P(None, "list", "leaf"),
            P("leaf"),
            P("leaf"),
            P(),
            P("list", None),
            P("leaf", None, None),
            P("leaf", "list", None),
            P("leaf", "list", None),
            P("leaf", "list"),
        ),
        out_specs=(P(None, ("leaf", "list")), P(None, "leaf")),
        check_vma=False,
    )
```

```python
import functools

import jax
import jax.numpy as jnp
from jax import lax
from jax.experimental import pallas as pl
from jax.experimental.pallas import tpu as pltpu
from jax.sharding import PartitionSpec as P

ORDER = 12
NCOEF = (ORDER + 1) ** 2
ROWS = 176
CHUNK = 48
LEAF = 256
CAP = 128
NEAR = 8
BATCH = 384
OCT = 8
WIDE = 256
HALF = ROWS // 2
BLOCK = 8
IN_PARTS = 4
ROWS_FIRST = 91
OPS_FIRST = 20
TREE = 48
TILES = 1 + NEAR * CAP // LEAF
PAIR = 4
SPREAD = 56

MESH = pl.DeviceIdType.MESH
F32 = jnp.float32
BF16 = jnp.bfloat16
NT = (((1,), (1,)), ((), ()))


def iota(shape, dim):
    return lax.broadcasted_iota(jnp.int32, shape, dim)


def onehot(mask):
    return jnp.where(mask, 1.0, 0.0).astype(BF16)


def dot(a, b):
    return jnp.dot(a, b, preferred_element_type=F32)


def dot_nt(a, b):
    return lax.dot_general(a, b, NT, preferred_element_type=F32)


def kernel(
    n_leaf,
    n_list,
    charge_hbm,
    position_hbm,
    count_hbm,
    octant_hbm,
    shift_hbm,
    m2l_hbm,
    let_hbm,
    src_hbm,
    dst_hbm,
    batch_hbm,
    local_out,
    tree_hbm,
    charge,
    position,
    count,
    octant,
    let_send,
    batch_count,
    tree_out,
    shift_ops,
    m2l_ops,
    list_src,
    list_dst,
    tz,
    tx,
    ty,
    acc,
    part,
    rs_buf,
    multi,
    outgoing,
    table,
    flat0,
    flat1,
    m_cat,
    s_cat,
    pick,
    x_own,
    x_buf,
    z_buf,
    total,
    fin,
    fin_buf,
    rs_send,
    rs_recv,
    ag_send,
    ag_recv,
    halo_send,
    halo_recv,
    fin_send,
    fin_recv,
    in_sem,
):
    n_ops = m2l_ops.shape[0]
    all_ops = SPREAD
    slots = charge.shape[0]
    me_leaf = lax.axis_index("leaf")
    me = lax.axis_index("list")
    offsets = [k - NEAR // 2 if k < NEAR // 2 else k - NEAR // 2 + 1 for k in range(NEAR)]
    near_ids = [lax.rem(me_leaf + off + n_leaf, n_leaf) for off in offsets]
    peers = [lax.rem(me + r, n_list) for r in range(1, n_list)]

    charges_in = [
        pltpu.make_async_copy(charge_hbm, charge, in_sem.at[0]),
        pltpu.make_async_copy(position_hbm, position, in_sem.at[1]),
        pltpu.make_async_copy(count_hbm, count, in_sem.at[5 + IN_PARTS]),
    ]
    step = m2l_ops.shape[1] // IN_PARTS
    ops_in = [
        pltpu.make_async_copy(
            m2l_hbm.at[:, i * step : i * step + step],
            m2l_ops.at[:, i * step : i * step + step],
            in_sem.at[5 + i],
        )
        for i in range(IN_PARTS)
    ]
    lists_in = [
        pltpu.make_async_copy(src_hbm, list_src, in_sem.at[3]),
        pltpu.make_async_copy(dst_hbm, list_dst, in_sem.at[4]),
        pltpu.make_async_copy(batch_hbm, batch_count, in_sem.at[6 + IN_PARTS]),
    ]
    cells_in = [
        pltpu.make_async_copy(let_hbm, let_send, in_sem.at[7 + IN_PARTS]),
        pltpu.make_async_copy(octant_hbm, octant, in_sem.at[8 + IN_PARTS]),
    ]
    ops_in.append(pltpu.make_async_copy(shift_hbm, shift_ops, in_sem.at[2]))
    for copy in charges_in + ops_in + lists_in + cells_in:
        copy.start()

    barrier = pltpu.get_barrier_semaphore()
    for near in near_ids:
        pl.semaphore_signal(barrier, inc=1, device_id=(near, me), device_id_type=MESH)
    for peer in peers:
        pl.semaphore_signal(barrier, inc=1, device_id=(me_leaf, peer), device_id_type=MESH)

    for copy in charges_in:
        copy.wait()
    slot_ids = me * slots + iota((slots, LEAF), 0)
    q = jnp.where(slot_ids < count[...], charge[...], 0.0)
    for axis, dst in ((0, tx), (1, ty), (2, tz)):
        v = position[axis]
        scale = q if axis == 2 else jnp.ones_like(v)
        prev, cur = scale, v * scale
        dst[0] = prev
        dst[1] = cur
        for n in range(2, ORDER + 1):
            prev, cur = cur, 2.0 * v * cur - prev
            dst[n] = cur
    for lane in range(LEAF // 128):
        cols = slice(lane * 128, lane * 128 + 128)
        acc[lane, NCOEF * 8 :, :] = jnp.zeros((acc.shape[1] - NCOEF * 8, 128), F32)
        for n in range(ORDER + 1):
            zn = tz[n, :, cols]
            for m in range(-n, n + 1):
                c = n * n + n + m
                if m > 0:
                    term = zn * tx[m, :, cols]
                elif m < 0:
                    term = zn * ty[-m, :, cols]
                else:
                    term = zn
                acc[lane, c * 8 : c * 8 + 8, :] = jnp.sum(term.reshape(slots // 8, 8, 128), axis=0)
        for chunk in range(n_list):
            s = acc[lane, pl.ds(chunk * CHUNK * 8, CHUNK, stride=8), :]
            for i in range(1, 8):
                s = s + acc[lane, pl.ds(chunk * CHUNK * 8 + i, CHUNK, stride=8), :]
            part[chunk, :, cols] = s

    pl.semaphore_wait(barrier, NEAR + n_list - 1)

    rs = []
    for r in range(1, n_list):
        copy = pltpu.make_async_remote_copy(
            src_ref=part.at[peers[r - 1]],
            dst_ref=rs_buf.at[r - 1],
            send_sem=rs_send.at[r - 1],
            recv_sem=rs_recv.at[r - 1],
            device_id=(me_leaf, peers[r - 1]),
            device_id_type=MESH,
        )
        copy.start()
        rs.append(copy)

    tail = pl.ds(NCOEF * all_ops, (ROWS - NCOEF) * all_ops)
    flat0[tail, :] = jnp.zeros(((ROWS - NCOEF) * all_ops, 128), F32)
    flat1[tail, :] = jnp.zeros(((ROWS - NCOEF) * all_ops, 128), F32)

    def align_rows(ks):
        for k in ks:
            first, turn = divmod(k * NCOEF, 128)
            for ref, at in ((m2l_ops, 0), (shift_ops, n_ops)):
                count_ops = ref.shape[0]
                lanes = iota((count_ops, 128), 1)
                pieces = []
                for i in range(2 if turn + NCOEF <= 256 else 3):
                    piece = ref[:, (first + i) * 128 : (first + i + 1) * 128].astype(F32)
                    pieces.append(pltpu.roll(piece, 128 - turn, 1) if turn else piece)
                keep = lanes < 128 - turn
                rest = pieces[1] if len(pieces) == 2 else jnp.where(keep, pieces[1], pieces[2])
                rows = slice(k * all_ops + at, k * all_ops + at + count_ops)
                flat0[rows, :] = jnp.where(keep, pieces[0], pieces[1])
                flat1[rows, :] = jnp.where(lanes < NCOEF - 128, rest, 0.0)

    for copy in ops_in:
        copy.wait()
    align_rows(range(ROWS_FIRST))

    for copy in rs:
        copy.wait()
    mine = part[me]
    for r in range(1, n_list):
        mine = mine + rs_buf[r - 1]
    multi[me] = mine.astype(BF16)
    ag = []
    for r in range(1, n_list):
        copy = pltpu.make_async_remote_copy(
            src_ref=multi.at[me],
            dst_ref=multi.at[me],
            send_sem=ag_send.at[r - 1],
            recv_sem=ag_recv.at[r - 1],
            device_id=(me_leaf, peers[r - 1]),
            device_id_type=MESH,
        )
        copy.start()
        ag.append(copy)

    align_rows(range(ROWS_FIRST, NCOEF))

    def take_op(g, _):
        cols = pl.multiple_of(g * WIDE, WIDE)
        m_cat[:, pl.ds(cols, 128)] = flat0[pl.ds(g, ROWS, stride=all_ops), :].astype(BF16)
        m_cat[:, pl.ds(cols + 128, 128)] = flat1[pl.ds(g, ROWS, stride=all_ops), :].astype(BF16)
        return 0

    lax.fori_loop(0, OPS_FIRST, take_op, 0, unroll=4)

    for copy in cells_in:
        copy.wait()
    for copy in ag:
        copy.wait()
    leaves = multi[...].reshape(n_list * CHUNK, LEAF)[:ROWS]
    table[0] = leaves

    halo = []
    for k in (0, 7, 1, 6, 2, 5, 3, 4):
        pickers = onehot(iota((LEAF, CAP), 0) == let_send[k : k + 1, :])
        outgoing[k] = dot(leaves, pickers).astype(BF16)
        to = NEAR - 1 - k
        copy = pltpu.make_async_remote_copy(
            src_ref=outgoing.at[k],
            dst_ref=table.at[1 + to // 2, :, to % 2 * CAP : to % 2 * CAP + CAP],
            send_sem=halo_send.at[k],
            recv_sem=halo_recv.at[k],
            device_id=(near_ids[k], me),
            device_id_type=MESH,
        )
        copy.start()
        halo.append(copy)

    lax.fori_loop(OPS_FIRST, n_ops, take_op, 0, unroll=4)
    for o in range(OCT):
        rows = pl.ds(n_ops + o, ROWS, stride=all_ops)
        s_cat[:, o * WIDE : o * WIDE + 128] = flat0[rows, :].astype(BF16)
        s_cat[:, o * WIDE + 128 : o * WIDE + 256] = flat1[rows, :].astype(BF16)

    pick[...] = jnp.zeros_like(pick)
    child = iota((128, LEAF), 1)
    cell = iota((128, LEAF), 0)
    octs = octant[pl.ds(0, LEAF)].reshape(1, LEAF)
    for o in range(OCT):
        chosen = onehot(cell == jnp.where(octs == o, child // 8, -1))
        pick[o * WIDE : o * WIDE + ROWS, :] = dot_nt(leaves, chosen).astype(BF16)
    parents = dot(s_cat[...], pick[...]).astype(BF16)
    n_par = LEAF // 8
    child = iota((128, n_par), 1)
    cell = iota((128, n_par), 0)
    octs = octant[pl.ds(LEAF, n_par)].reshape(1, n_par)
    for o in range(OCT):
        chosen = onehot(cell == jnp.where(octs == o, n_par + child // 8, -1))
        pick[o * WIDE : o * WIDE + ROWS, :] = dot_nt(parents[:, :n_par], chosen).astype(BF16)
    grand = dot(s_cat[...], pick[...])
    tree = jnp.where(iota((ROWS, 128), 1) < n_par, parents.astype(F32), grand)
    tree_out[...] = tree.T[:TREE, :NCOEF].astype(BF16)
    tree_done = pltpu.make_async_copy(tree_out, tree_hbm, in_sem.at[9 + IN_PARTS])
    tree_done.start()


    for copy in lists_in:
        copy.wait()

    def hot16(row, base, n):
        ids = iota((n, row.shape[1]), 0).astype(jnp.int16)
        return jnp.where(ids == (row - base).astype(jnp.int16), jnp.array(1, BF16), jnp.array(0, BF16))

    def sources(g):
        rows = []
        for v in range(PAIR):
            src = list_src[pl.ds(g + v, 1), :]
            rows.append(jnp.where(iota((1, BATCH), 1) < batch_count[0, g + v], src, TILES * LEAF))
        return jnp.concatenate(rows, axis=1)

    def gather_own(p, _):
        x_own[p] = dot(leaves, hot16(sources(p * PAIR), 0, LEAF)).astype(BF16)
        return 0

    lax.fori_loop(0, n_ops // PAIR, gather_own, 0, unroll=4)
    for copy in halo:
        copy.wait()

    def gather(i):
        for u in range(0, BLOCK, PAIR):
            src = sources(i * BLOCK + u)
            tile = src // LEAF
            others = table[1:].reshape((TILES - 1) * ROWS, LEAF)
            each = dot(others, hot16(src - tile * LEAF, 0, LEAF))
            x = x_own[i * (BLOCK // PAIR) + u // PAIR].astype(F32)
            for h in range(1, TILES):
                x = jnp.where(tile == h, each[(h - 1) * ROWS : h * ROWS], x)
            for v in range(PAIR):
                x_buf[lax.rem(i, 2), u + v] = x[:, v * BATCH : v * BATCH + BATCH].astype(BF16)

    def scatter(i):
        for u in range(BLOCK):
            dst = list_dst[pl.ds(i * BLOCK + u, 1), :]
            z = dot_nt(x_buf[lax.rem(i, 2), u], hot16(dst, 0, LEAF))
            z_buf[lax.rem(i, 2), u * WIDE : u * WIDE + ROWS, :] = z.astype(BF16)

    def apply(i):
        cols = pl.ds(pl.multiple_of(i * (BLOCK * WIDE), BLOCK * WIDE), BLOCK * WIDE)
        total[...] += dot(m_cat[:, cols], z_buf[lax.rem(i, 2)])

    blocks = n_ops // BLOCK
    total[...] = jnp.zeros_like(total)
    z_buf[...] = jnp.zeros_like(z_buf)
    gather(jnp.int32(0))
    scatter(jnp.int32(0))
    gather(jnp.int32(1))

    def steps(i, _):
        apply(i - 2)
        scatter(i - 1)
        gather(i)
        return 0

    lax.fori_loop(2, blocks, steps, 0)
    apply(jnp.int32(blocks - 2))
    scatter(jnp.int32(blocks - 1))
    apply(jnp.int32(blocks - 1))

    left = iota((HALF, 128), 1) < 64
    for j in range(n_list):
        cols = slice(j // 2 * 128, j // 2 * 128 + 128)
        top, low = total[:HALF, cols], total[HALF:, cols]
        if j % 2 == 0:
            fin[j] = jnp.where(left, top, pltpu.roll(low, 64, 1))
        else:
            fin[j] = jnp.where(left, pltpu.roll(top, 64, 1), low)
    last = []
    for r in range(1, n_list):
        copy = pltpu.make_async_remote_copy(
            src_ref=fin.at[peers[r - 1]],
            dst_ref=fin_buf.at[r - 1],
            send_sem=fin_send.at[r - 1],
            recv_sem=fin_recv.at[r - 1],
            device_id=(me_leaf, peers[r - 1]),
            device_id_type=MESH,
        )
        copy.start()
        last.append(copy)
    for copy in last:
        copy.wait()
    s = fin[me]
    for r in range(1, n_list):
        s = s + fin_buf[r - 1]
    s = jnp.concatenate([s, pltpu.roll(s, 64, 1)], axis=0)
    local_out[...] = s.T[: local_out.shape[0], :NCOEF].astype(BF16)
    tree_done.wait()


def finish(local, tree, local_out, tree_out):
    local_out[...] = local[...]
    tree_out[...] = tree[: tree_out.shape[0], :]


def per_device(
    n_leaf,
    n_list,
    charge,
    position,
    charge_count,
    octant,
    shift_ops,
    m2l_ops,
    let_send,
    list_src,
    list_dst,
    batch_count,
):
    slots = charge.shape[0]
    n_ops = m2l_ops.shape[0]
    all_ops = SPREAD
    vmem = pl.BlockSpec(memory_space=pltpu.VMEM)
    dma = pltpu.SemaphoreType.DMA
    hbm = pl.BlockSpec(memory_space=pl.ANY)
    local, tree = pl.pallas_call(
        functools.partial(kernel, n_leaf, n_list),
        out_shape=(
            jax.ShapeDtypeStruct((LEAF // n_list, NCOEF), BF16),
            jax.ShapeDtypeStruct((TREE, NCOEF), BF16),
        ),
        in_specs=[hbm] * 10,
        out_specs=(vmem, hbm),
        scratch_shapes=[
            pltpu.VMEM(charge.shape, F32),
            pltpu.VMEM(position.shape, F32),
            pltpu.VMEM((1, LEAF), jnp.int32),
            pltpu.VMEM(octant.shape, jnp.int32),
            pltpu.VMEM(let_send.shape[1:], jnp.int32),
            pltpu.SMEM(batch_count.shape, jnp.int32),
            pltpu.VMEM((TREE, NCOEF), BF16),
            pltpu.VMEM(shift_ops.shape, BF16),
            pltpu.VMEM(m2l_ops.shape, BF16),
            pltpu.VMEM(list_src.shape[1:], jnp.int32),
            pltpu.VMEM(list_src.shape[1:], jnp.int32),
            pltpu.VMEM((ORDER + 1, slots, LEAF), F32),
            pltpu.VMEM((ORDER + 1, slots, LEAF), F32),
            pltpu.VMEM((ORDER + 1, slots, LEAF), F32),
            pltpu.VMEM((LEAF // 128, n_list * CHUNK * 8, 128), F32),
            pltpu.VMEM((n_list, CHUNK, LEAF), F32),
            pltpu.VMEM((n_list - 1, CHUNK, LEAF), F32),
            pltpu.VMEM((n_list, CHUNK, LEAF), BF16),
            pltpu.VMEM((NEAR, ROWS, CAP), BF16),
            pltpu.VMEM((TILES, ROWS, LEAF), BF16),
            pltpu.VMEM((ROWS * all_ops, 128), F32),
            pltpu.VMEM((ROWS * all_ops, 128), F32),
            pltpu.VMEM((ROWS, n_ops * WIDE), BF16),
            pltpu.VMEM((ROWS, OCT * WIDE), BF16),
            pltpu.VMEM((OCT * WIDE, 128), BF16),
            pltpu.VMEM((n_ops // PAIR, ROWS, PAIR * BATCH), BF16),
            pltpu.VMEM((2, BLOCK, ROWS, BATCH), BF16),
            pltpu.VMEM((2, BLOCK * WIDE, LEAF), BF16),
            pltpu.VMEM((ROWS, LEAF), F32),
            pltpu.VMEM((n_list, HALF, 128), F32),
            pltpu.VMEM((n_list - 1, HALF, 128), F32),
            dma((n_list - 1,)),
            dma((n_list - 1,)),
            dma((n_list - 1,)),
            dma((n_list - 1,)),
            dma((NEAR,)),
            dma((NEAR,)),
            dma((n_list - 1,)),
            dma((n_list - 1,)),
            dma((10 + IN_PARTS,)),
        ],
        compiler_params=pltpu.CompilerParams(
            collective_id=0, has_side_effects=True, vmem_limit_bytes=56 << 20
        ),
    )(
        charge,
        position,
        charge_count.reshape(1, -1),
        octant,
        shift_ops,
        m2l_ops,
        let_send[0],
        list_src[0],
        list_dst[0],
        batch_count,
    )
    local_t, tree_t = pl.pallas_call(
        finish,
        out_shape=(
            jax.ShapeDtypeStruct((LEAF // n_list, NCOEF), BF16),
            jax.ShapeDtypeStruct((LEAF // 8 + LEAF // 64, NCOEF), BF16),
        ),
        in_specs=[vmem, vmem],
        out_specs=(vmem, vmem),
    )(local, tree)
    return local_t.T, tree_t.T


def solution(mesh):
    return jax.shard_map(
        functools.partial(per_device, mesh.shape["leaf"], mesh.shape["list"]),
        mesh=mesh,
        in_specs=(
            P("list", "leaf"),
            P(None, "list", "leaf"),
            P("leaf"),
            P("leaf"),
            P(),
            P("list", None),
            P("leaf", None, None),
            P("leaf", "list", None),
            P("leaf", "list", None),
            P("leaf", "list"),
        ),
        out_specs=(P(None, ("leaf", "list")), P(None, "leaf")),
        check_vma=False,
    )
```

```python
import functools

import jax
import jax.numpy as jnp
from jax import lax
from jax.experimental import pallas as pl
from jax.experimental.pallas import tpu as pltpu
from jax.sharding import PartitionSpec as P

ORDER = 12
NCOEF = (ORDER + 1) ** 2
ROWS = 176
CHUNK = 48
LEAF = 256
CAP = 128
NEAR = 8
BATCH = 384
OCT = 8
WIDE = 256
HALF = ROWS // 2
BLOCK = 8
IN_PARTS = 4
ROWS_FIRST = 91
OPS_FIRST = 20
TREE = 48
TILES = 1 + NEAR * CAP // LEAF
PAIR = 2
SPREAD = 56

MESH = pl.DeviceIdType.MESH
F32 = jnp.float32
BF16 = jnp.bfloat16
NT = (((1,), (1,)), ((), ()))


def iota(shape, dim):
    return lax.broadcasted_iota(jnp.int32, shape, dim)


def onehot(mask):
    return jnp.where(mask, 1.0, 0.0).astype(BF16)


def hot16(row, base, n):
    ids = iota((n, row.shape[1]), 0).astype(jnp.int16)
    return jnp.where(ids == (row - base).astype(jnp.int16), jnp.array(1, BF16), jnp.array(0, BF16))


def dot(a, b):
    return jnp.dot(a, b, preferred_element_type=F32)


def dot_nt(a, b):
    return lax.dot_general(a, b, NT, preferred_element_type=F32)


def kernel(
    n_leaf,
    n_list,
    charge_hbm,
    position_hbm,
    count_hbm,
    octant_hbm,
    shift_hbm,
    m2l_hbm,
    let_hbm,
    src_hbm,
    dst_hbm,
    batch_hbm,
    local_out,
    tree_hbm,
    charge,
    position,
    count,
    octant,
    let_send,
    batch_count,
    tree_out,
    shift_ops,
    m2l_ops,
    list_src,
    list_dst,
    tz,
    tx,
    ty,
    acc,
    part,
    rs_buf,
    multi,
    pickers,
    outgoing,
    table,
    flat0,
    flat1,
    m_cat,
    s_cat,
    pick,
    x_own,
    x_buf,
    z_buf,
    total,
    fin,
    fin_buf,
    rs_send,
    rs_recv,
    ag_send,
    ag_recv,
    halo_send,
    halo_recv,
    fin_send,
    fin_recv,
    in_sem,
):
    n_ops = m2l_ops.shape[0]
    all_ops = SPREAD
    slots = charge.shape[0]
    me_leaf = lax.axis_index("leaf")
    me = lax.axis_index("list")
    offsets = [k - NEAR // 2 if k < NEAR // 2 else k - NEAR // 2 + 1 for k in range(NEAR)]
    near_ids = [lax.rem(me_leaf + off + n_leaf, n_leaf) for off in offsets]
    peers = [lax.rem(me + r, n_list) for r in range(1, n_list)]
    far_first = sorted(range(1, n_list), key=lambda r: -min(r, n_list - r))

    charges_in = [
        pltpu.make_async_copy(charge_hbm, charge, in_sem.at[0]),
        pltpu.make_async_copy(position_hbm, position, in_sem.at[1]),
        pltpu.make_async_copy(count_hbm, count, in_sem.at[5 + IN_PARTS]),
    ]
    step = m2l_ops.shape[1] // IN_PARTS
    ops_in = [
        pltpu.make_async_copy(
            m2l_hbm.at[:, i * step : i * step + step],
            m2l_ops.at[:, i * step : i * step + step],
            in_sem.at[5 + i],
        )
        for i in range(IN_PARTS)
    ]
    lists_in = [
        pltpu.make_async_copy(src_hbm, list_src, in_sem.at[3]),
        pltpu.make_async_copy(dst_hbm, list_dst, in_sem.at[4]),
        pltpu.make_async_copy(batch_hbm, batch_count, in_sem.at[6 + IN_PARTS]),
    ]
    cells_in = [
        pltpu.make_async_copy(let_hbm, let_send, in_sem.at[7 + IN_PARTS]),
        pltpu.make_async_copy(octant_hbm, octant, in_sem.at[8 + IN_PARTS]),
    ]
    ops_in.append(pltpu.make_async_copy(shift_hbm, shift_ops, in_sem.at[2]))
    for copy in charges_in + ops_in + lists_in + cells_in:
        copy.start()

    barrier = pltpu.get_barrier_semaphore()
    for near in near_ids:
        pl.semaphore_signal(barrier, inc=1, device_id=(near, me), device_id_type=MESH)
    for peer in peers:
        pl.semaphore_signal(barrier, inc=1, device_id=(me_leaf, peer), device_id_type=MESH)

    for copy in charges_in:
        copy.wait()
    slot_ids = me * slots + iota((slots, LEAF), 0)
    q = jnp.where(slot_ids < count[...], charge[...], 0.0)
    for axis, dst in ((0, tx), (1, ty), (2, tz)):
        v = position[axis]
        scale = q if axis == 2 else jnp.ones_like(v)
        prev, cur = scale, v * scale
        dst[0] = prev
        dst[1] = cur
        for n in range(2, ORDER + 1):
            prev, cur = cur, 2.0 * v * cur - prev
            dst[n] = cur
    for lane in range(LEAF // 128):
        cols = slice(lane * 128, lane * 128 + 128)
        acc[lane, NCOEF * 8 :, :] = jnp.zeros((acc.shape[1] - NCOEF * 8, 128), F32)
        for n in range(ORDER + 1):
            zn = tz[n, :, cols]
            for m in range(-n, n + 1):
                c = n * n + n + m
                if m > 0:
                    term = zn * tx[m, :, cols]
                elif m < 0:
                    term = zn * ty[-m, :, cols]
                else:
                    term = zn
                acc[lane, c * 8 : c * 8 + 8, :] = jnp.sum(term.reshape(slots // 8, 8, 128), axis=0)
        for chunk in range(n_list):
            s = acc[lane, pl.ds(chunk * CHUNK * 8, CHUNK, stride=8), :]
            for i in range(1, 8):
                s = s + acc[lane, pl.ds(chunk * CHUNK * 8 + i, CHUNK, stride=8), :]
            part[chunk, :, cols] = s

    pl.semaphore_wait(barrier, NEAR + n_list - 1)

    rs = []
    for r in far_first:
        copy = pltpu.make_async_remote_copy(
            src_ref=part.at[peers[r - 1]],
            dst_ref=rs_buf.at[r - 1],
            send_sem=rs_send.at[r - 1],
            recv_sem=rs_recv.at[r - 1],
            device_id=(me_leaf, peers[r - 1]),
            device_id_type=MESH,
        )
        copy.start()
        rs.append(copy)

    tail = pl.ds(NCOEF * all_ops, (ROWS - NCOEF) * all_ops)
    flat0[tail, :] = jnp.zeros(((ROWS - NCOEF) * all_ops, 128), F32)
    flat1[tail, :] = jnp.zeros(((ROWS - NCOEF) * all_ops, 128), F32)

    def align_rows(ks):
        for k in ks:
            first, turn = divmod(k * NCOEF, 128)
            for ref, at in ((m2l_ops, 0), (shift_ops, n_ops)):
                count_ops = ref.shape[0]
                lanes = iota((count_ops, 128), 1)
                pieces = []
                for i in range(2 if turn + NCOEF <= 256 else 3):
                    piece = ref[:, (first + i) * 128 : (first + i + 1) * 128].astype(F32)
                    pieces.append(pltpu.roll(piece, 128 - turn, 1) if turn else piece)
                keep = lanes < 128 - turn
                rest = pieces[1] if len(pieces) == 2 else jnp.where(keep, pieces[1], pieces[2])
                rows = slice(k * all_ops + at, k * all_ops + at + count_ops)
                flat0[rows, :] = jnp.where(keep, pieces[0], pieces[1])
                flat1[rows, :] = jnp.where(lanes < NCOEF - 128, rest, 0.0)

    for copy in ops_in:
        copy.wait()
    align_rows(range(ROWS_FIRST))

    for copy in rs:
        copy.wait()
    mine = part[me]
    for r in range(1, n_list):
        mine = mine + rs_buf[r - 1]
    multi[me] = mine.astype(BF16)
    ag = []
    for r in far_first:
        copy = pltpu.make_async_remote_copy(
            src_ref=multi.at[me],
            dst_ref=multi.at[me],
            send_sem=ag_send.at[r - 1],
            recv_sem=ag_recv.at[r - 1],
            device_id=(me_leaf, peers[r - 1]),
            device_id_type=MESH,
        )
        copy.start()
        ag.append(copy)

    align_rows(range(ROWS_FIRST, NCOEF))

    def take_op(g, _):
        cols = pl.multiple_of(g * WIDE, WIDE)
        m_cat[:, pl.ds(cols, 128)] = flat0[pl.ds(g, ROWS, stride=all_ops), :].astype(BF16)
        m_cat[:, pl.ds(cols + 128, 128)] = flat1[pl.ds(g, ROWS, stride=all_ops), :].astype(BF16)
        return 0

    lax.fori_loop(0, OPS_FIRST, take_op, 0, unroll=4)

    for copy in cells_in:
        copy.wait()
    for k in range(NEAR):
        pickers[:, k * CAP : k * CAP + CAP] = hot16(let_send[k : k + 1, :], 0, LEAF)
    for copy in ag:
        copy.wait()
    leaves = multi[...].reshape(n_list * CHUNK, LEAF)[:ROWS]
    table[0] = leaves

    picked = dot(leaves, pickers[...]).astype(BF16)
    halo = []
    for k in (0, 7, 1, 6, 2, 5, 3, 4):
        outgoing[k] = picked[:, k * CAP : k * CAP + CAP]
        to = NEAR - 1 - k
        copy = pltpu.make_async_remote_copy(
            src_ref=outgoing.at[k],
            dst_ref=table.at[1 + to // 2, :, to % 2 * CAP : to % 2 * CAP + CAP],
            send_sem=halo_send.at[k],
            recv_sem=halo_recv.at[k],
            device_id=(near_ids[k], me),
            device_id_type=MESH,
        )
        copy.start()
        halo.append(copy)

    lax.fori_loop(OPS_FIRST, n_ops, take_op, 0, unroll=4)
    for copy in lists_in:
        copy.wait()

    def sources(g):
        rows = []
        for v in range(PAIR):
            src = list_src[pl.ds(g + v, 1), :]
            rows.append(jnp.where(iota((1, BATCH), 1) < batch_count[0, g + v], src, TILES * LEAF))
        return jnp.concatenate(rows, axis=1)

    def gather_own(p, _):
        x_own[p] = dot(leaves, hot16(sources(p * PAIR), 0, LEAF)).astype(BF16)
        return 0

    lax.fori_loop(0, n_ops // PAIR, gather_own, 0, unroll=4)
    for copy in halo:
        copy.wait()

    def gather(i):
        for u in range(0, BLOCK, PAIR):
            src = sources(i * BLOCK + u)
            tile = src // LEAF
            others = table[1:].reshape((TILES - 1) * ROWS, LEAF)
            each = dot(others, hot16(src - tile * LEAF, 0, LEAF))
            x = x_own[i * (BLOCK // PAIR) + u // PAIR].astype(F32)
            for h in range(1, TILES):
                x = jnp.where(tile == h, each[(h - 1) * ROWS : h * ROWS], x)
            for v in range(PAIR):
                x_buf[lax.rem(i, 2), u + v] = x[:, v * BATCH : v * BATCH + BATCH].astype(BF16)

    def scatter(i):
        for u in range(BLOCK):
            dst = list_dst[pl.ds(i * BLOCK + u, 1), :]
            z = dot_nt(x_buf[lax.rem(i, 2), u], hot16(dst, 0, LEAF))
            z_buf[lax.rem(i, 2), u * WIDE : u * WIDE + ROWS, :] = z.astype(BF16)

    def apply(i):
        cols = pl.ds(pl.multiple_of(i * (BLOCK * WIDE), BLOCK * WIDE), BLOCK * WIDE)
        total[...] += dot(m_cat[:, cols], z_buf[lax.rem(i, 2)])

    blocks = n_ops // BLOCK
    total[...] = jnp.zeros_like(total)
    z_buf[...] = jnp.zeros_like(z_buf)
    gather(jnp.int32(0))
    scatter(jnp.int32(0))
    gather(jnp.int32(1))

    def steps(i, _):
        apply(i - 2)
        scatter(i - 1)
        gather(i)
        return 0

    lax.fori_loop(2, blocks, steps, 0)
    apply(jnp.int32(blocks - 2))
    scatter(jnp.int32(blocks - 1))
    apply(jnp.int32(blocks - 1))

    left = iota((HALF, 128), 1) < 64
    for j in range(n_list):
        cols = slice(j // 2 * 128, j // 2 * 128 + 128)
        top, low = total[:HALF, cols], total[HALF:, cols]
        if j % 2 == 0:
            fin[j] = jnp.where(left, top, pltpu.roll(low, 64, 1))
        else:
            fin[j] = jnp.where(left, pltpu.roll(top, 64, 1), low)
    last = []
    for r in far_first:
        copy = pltpu.make_async_remote_copy(
            src_ref=fin.at[peers[r - 1]],
            dst_ref=fin_buf.at[r - 1],
            send_sem=fin_send.at[r - 1],
            recv_sem=fin_recv.at[r - 1],
            device_id=(me_leaf, peers[r - 1]),
            device_id_type=MESH,
        )
        copy.start()
        last.append(copy)
    for o in range(OCT):
        rows = pl.ds(n_ops + o, ROWS, stride=all_ops)
        s_cat[:, o * WIDE : o * WIDE + 128] = flat0[rows, :].astype(BF16)
        s_cat[:, o * WIDE + 128 : o * WIDE + 256] = flat1[rows, :].astype(BF16)

    pick[...] = jnp.zeros_like(pick)
    child = iota((128, LEAF), 1)
    cell = iota((128, LEAF), 0)
    octs = octant[pl.ds(0, LEAF)].reshape(1, LEAF)
    for o in range(OCT):
        chosen = onehot(cell == jnp.where(octs == o, child // 8, -1))
        pick[o * WIDE : o * WIDE + ROWS, :] = dot_nt(leaves, chosen).astype(BF16)
    parents = dot(s_cat[...], pick[...]).astype(BF16)
    n_par = LEAF // 8
    child = iota((128, n_par), 1)
    cell = iota((128, n_par), 0)
    octs = octant[pl.ds(LEAF, n_par)].reshape(1, n_par)
    for o in range(OCT):
        chosen = onehot(cell == jnp.where(octs == o, n_par + child // 8, -1))
        pick[o * WIDE : o * WIDE + ROWS, :] = dot_nt(parents[:, :n_par], chosen).astype(BF16)
    grand = dot(s_cat[...], pick[...])
    tree = jnp.where(iota((ROWS, 128), 1) < n_par, parents.astype(F32), grand)
    tree_out[...] = tree.T[:TREE, :NCOEF].astype(BF16)
    tree_done = pltpu.make_async_copy(tree_out, tree_hbm, in_sem.at[9 + IN_PARTS])
    tree_done.start()


    for copy in last:
        copy.wait()
    s = fin[me]
    for r in range(1, n_list):
        s = s + fin_buf[r - 1]
    s = jnp.concatenate([s, pltpu.roll(s, 64, 1)], axis=0)
    local_out[...] = s.T[: local_out.shape[0], :NCOEF].astype(BF16)
    tree_done.wait()


def finish(local, tree, local_out, tree_out):
    local_out[...] = local[...]
    tree_out[...] = tree[: tree_out.shape[0], :]


def per_device(
    n_leaf,
    n_list,
    charge,
    position,
    charge_count,
    octant,
    shift_ops,
    m2l_ops,
    let_send,
    list_src,
    list_dst,
    batch_count,
):
    slots = charge.shape[0]
    n_ops = m2l_ops.shape[0]
    all_ops = SPREAD
    vmem = pl.BlockSpec(memory_space=pltpu.VMEM)
    dma = pltpu.SemaphoreType.DMA
    hbm = pl.BlockSpec(memory_space=pl.ANY)
    local, tree = pl.pallas_call(
        functools.partial(kernel, n_leaf, n_list),
        out_shape=(
            jax.ShapeDtypeStruct((LEAF // n_list, NCOEF), BF16),
            jax.ShapeDtypeStruct((TREE, NCOEF), BF16),
        ),
        in_specs=[hbm] * 10,
        out_specs=(vmem, hbm),
        scratch_shapes=[
            pltpu.VMEM(charge.shape, F32),
            pltpu.VMEM(position.shape, F32),
            pltpu.VMEM((1, LEAF), jnp.int32),
            pltpu.VMEM(octant.shape, jnp.int32),
            pltpu.VMEM(let_send.shape[1:], jnp.int32),
            pltpu.SMEM(batch_count.shape, jnp.int32),
            pltpu.VMEM((TREE, NCOEF), BF16),
            pltpu.VMEM(shift_ops.shape, BF16),
            pltpu.VMEM(m2l_ops.shape, BF16),
            pltpu.VMEM(list_src.shape[1:], jnp.int32),
            pltpu.VMEM(list_src.shape[1:], jnp.int32),
            pltpu.VMEM((ORDER + 1, slots, LEAF), F32),
            pltpu.VMEM((ORDER + 1, slots, LEAF), F32),
            pltpu.VMEM((ORDER + 1, slots, LEAF), F32),
            pltpu.VMEM((LEAF // 128, n_list * CHUNK * 8, 128), F32),
            pltpu.VMEM((n_list, CHUNK, LEAF), F32),
            pltpu.VMEM((n_list - 1, CHUNK, LEAF), F32),
            pltpu.VMEM((n_list, CHUNK, LEAF), BF16),
            pltpu.VMEM((LEAF, NEAR * CAP), BF16),
            pltpu.VMEM((NEAR, ROWS, CAP), BF16),
            pltpu.VMEM((TILES, ROWS, LEAF), BF16),
            pltpu.VMEM((ROWS * all_ops, 128), F32),
            pltpu.VMEM((ROWS * all_ops, 128), F32),
            pltpu.VMEM((ROWS, n_ops * WIDE), BF16),
            pltpu.VMEM((ROWS, OCT * WIDE), BF16),
            pltpu.VMEM((OCT * WIDE, 128), BF16),
            pltpu.VMEM((n_ops // PAIR, ROWS, PAIR * BATCH), BF16),
            pltpu.VMEM((2, BLOCK, ROWS, BATCH), BF16),
            pltpu.VMEM((2, BLOCK * WIDE, LEAF), BF16),
            pltpu.VMEM((ROWS, LEAF), F32),
            pltpu.VMEM((n_list, HALF, 128), F32),
            pltpu.VMEM((n_list - 1, HALF, 128), F32),
            dma((n_list - 1,)),
            dma((n_list - 1,)),
            dma((n_list - 1,)),
            dma((n_list - 1,)),
            dma((NEAR,)),
            dma((NEAR,)),
            dma((n_list - 1,)),
            dma((n_list - 1,)),
            dma((10 + IN_PARTS,)),
        ],
        compiler_params=pltpu.CompilerParams(
            collective_id=0, has_side_effects=True, vmem_limit_bytes=56 << 20
        ),
    )(
        charge,
        position,
        charge_count.reshape(1, -1),
        octant,
        shift_ops,
        m2l_ops,
        let_send[0],
        list_src[0],
        list_dst[0],
        batch_count,
    )
    local_t, tree_t = pl.pallas_call(
        finish,
        out_shape=(
            jax.ShapeDtypeStruct((LEAF // n_list, NCOEF), BF16),
            jax.ShapeDtypeStruct((LEAF // 8 + LEAF // 64, NCOEF), BF16),
        ),
        in_specs=[vmem, vmem],
        out_specs=(vmem, vmem),
    )(local, tree)
    return local_t.T, tree_t.T


def solution(mesh):
    return jax.shard_map(
        functools.partial(per_device, mesh.shape["leaf"], mesh.shape["list"]),
        mesh=mesh,
        in_specs=(
            P("list", "leaf"),
            P(None, "list", "leaf"),
            P("leaf"),
            P("leaf"),
            P(),
            P("list", None),
            P("leaf", None, None),
            P("leaf", "list", None),
            P("leaf", "list", None),
            P("leaf", "list"),
        ),
        out_specs=(P(None, ("leaf", "list")), P(None, "leaf")),
        check_vma=False,
    )
```

```python
import functools

import jax
import jax.numpy as jnp
from jax import lax
from jax.experimental import pallas as pl
from jax.experimental.pallas import tpu as pltpu
from jax.sharding import PartitionSpec as P

ORDER = 12
NCOEF = (ORDER + 1) ** 2
ROWS = 176
CHUNK = 48
LEAF = 256
CAP = 128
NEAR = 8
BATCH = 384
OCT = 8
WIDE = 256
HALF = ROWS // 2
BLOCK = 10
IN_PARTS = 4
ROWS_FIRST = 91
OPS_FIRST = 20
TREE = 48
TILES = 1 + NEAR * CAP // LEAF
PAIR = 2
SPREAD = 56

MESH = pl.DeviceIdType.MESH
F32 = jnp.float32
BF16 = jnp.bfloat16
NT = (((1,), (1,)), ((), ()))


def iota(shape, dim):
    return lax.broadcasted_iota(jnp.int32, shape, dim)


def onehot(mask):
    return jnp.where(mask, 1.0, 0.0).astype(BF16)


def hot16(row, base, n):
    ids = iota((n, row.shape[1]), 0).astype(jnp.int16)
    return jnp.where(ids == (row - base).astype(jnp.int16), jnp.array(1, BF16), jnp.array(0, BF16))


def dot(a, b):
    return jnp.dot(a, b, preferred_element_type=F32)


def dot_nt(a, b):
    return lax.dot_general(a, b, NT, preferred_element_type=F32)


def kernel(
    n_leaf,
    n_list,
    charge_hbm,
    position_hbm,
    count_hbm,
    octant_hbm,
    shift_hbm,
    m2l_hbm,
    let_hbm,
    src_hbm,
    dst_hbm,
    batch_hbm,
    local_out,
    tree_hbm,
    charge,
    position,
    count,
    octant,
    let_send,
    batch_count,
    tree_out,
    shift_ops,
    m2l_ops,
    list_src,
    list_dst,
    tz,
    tx,
    ty,
    acc,
    part,
    rs_buf,
    multi,
    pickers,
    outgoing,
    table,
    flat0,
    flat1,
    m_cat,
    s_cat,
    pick,
    x_own,
    x_buf,
    z_buf,
    total,
    fin,
    fin_buf,
    rs_send,
    rs_recv,
    ag_send,
    ag_recv,
    halo_send,
    halo_recv,
    fin_send,
    fin_recv,
    in_sem,
):
    n_ops = m2l_ops.shape[0]
    all_ops = SPREAD
    slots = charge.shape[0]
    me_leaf = lax.axis_index("leaf")
    me = lax.axis_index("list")
    offsets = [k - NEAR // 2 if k < NEAR // 2 else k - NEAR // 2 + 1 for k in range(NEAR)]
    near_ids = [lax.rem(me_leaf + off + n_leaf, n_leaf) for off in offsets]
    peers = [lax.rem(me + r, n_list) for r in range(1, n_list)]
    far_first = sorted(range(1, n_list), key=lambda r: -min(r, n_list - r))

    charges_in = [
        pltpu.make_async_copy(charge_hbm, charge, in_sem.at[0]),
        pltpu.make_async_copy(position_hbm, position, in_sem.at[1]),
        pltpu.make_async_copy(count_hbm, count, in_sem.at[5 + IN_PARTS]),
    ]
    step = m2l_ops.shape[1] // IN_PARTS
    ops_in = [
        pltpu.make_async_copy(
            m2l_hbm.at[:, i * step : i * step + step],
            m2l_ops.at[:, i * step : i * step + step],
            in_sem.at[5 + i],
        )
        for i in range(IN_PARTS)
    ]
    lists_in = [
        pltpu.make_async_copy(src_hbm, list_src, in_sem.at[3]),
        pltpu.make_async_copy(dst_hbm, list_dst, in_sem.at[4]),
        pltpu.make_async_copy(batch_hbm, batch_count, in_sem.at[6 + IN_PARTS]),
    ]
    cells_in = [
        pltpu.make_async_copy(let_hbm, let_send, in_sem.at[7 + IN_PARTS]),
        pltpu.make_async_copy(octant_hbm, octant, in_sem.at[8 + IN_PARTS]),
    ]
    ops_in.append(pltpu.make_async_copy(shift_hbm, shift_ops, in_sem.at[2]))
    for copy in charges_in + ops_in + lists_in + cells_in:
        copy.start()

    barrier = pltpu.get_barrier_semaphore()
    for near in near_ids:
        pl.semaphore_signal(barrier, inc=1, device_id=(near, me), device_id_type=MESH)
    for peer in peers:
        pl.semaphore_signal(barrier, inc=1, device_id=(me_leaf, peer), device_id_type=MESH)

    for copy in charges_in:
        copy.wait()
    slot_ids = me * slots + iota((slots, LEAF), 0)
    q = jnp.where(slot_ids < count[...], charge[...], 0.0)
    for axis, dst in ((0, tx), (1, ty), (2, tz)):
        v = position[axis]
        scale = q if axis == 2 else jnp.ones_like(v)
        prev, cur = scale, v * scale
        dst[0] = prev
        dst[1] = cur
        for n in range(2, ORDER + 1):
            prev, cur = cur, 2.0 * v * cur - prev
            dst[n] = cur
    for lane in range(LEAF // 128):
        cols = slice(lane * 128, lane * 128 + 128)
        acc[lane, NCOEF * 8 :, :] = jnp.zeros((acc.shape[1] - NCOEF * 8, 128), F32)
        for n in range(ORDER + 1):
            zn = tz[n, :, cols]
            for m in range(-n, n + 1):
                c = n * n + n + m
                if m > 0:
                    term = zn * tx[m, :, cols]
                elif m < 0:
                    term = zn * ty[-m, :, cols]
                else:
                    term = zn
                acc[lane, c * 8 : c * 8 + 8, :] = jnp.sum(term.reshape(slots // 8, 8, 128), axis=0)
        for chunk in range(n_list):
            s = acc[lane, pl.ds(chunk * CHUNK * 8, CHUNK, stride=8), :]
            for i in range(1, 8):
                s = s + acc[lane, pl.ds(chunk * CHUNK * 8 + i, CHUNK, stride=8), :]
            part[chunk, :, cols] = s

    pl.semaphore_wait(barrier, NEAR + n_list - 1)

    rs = []
    for r in far_first:
        copy = pltpu.make_async_remote_copy(
            src_ref=part.at[peers[r - 1]],
            dst_ref=rs_buf.at[r - 1],
            send_sem=rs_send.at[r - 1],
            recv_sem=rs_recv.at[r - 1],
            device_id=(me_leaf, peers[r - 1]),
            device_id_type=MESH,
        )
        copy.start()
        rs.append(copy)

    tail = pl.ds(NCOEF * all_ops, (ROWS - NCOEF) * all_ops)
    flat0[tail, :] = jnp.zeros(((ROWS - NCOEF) * all_ops, 128), F32)
    flat1[tail, :] = jnp.zeros(((ROWS - NCOEF) * all_ops, 128), F32)

    def align_rows(ks):
        for k in ks:
            first, turn = divmod(k * NCOEF, 128)
            for ref, at in ((m2l_ops, 0), (shift_ops, n_ops)):
                count_ops = ref.shape[0]
                lanes = iota((count_ops, 128), 1)
                pieces = []
                for i in range(2 if turn + NCOEF <= 256 else 3):
                    piece = ref[:, (first + i) * 128 : (first + i + 1) * 128].astype(F32)
                    pieces.append(pltpu.roll(piece, 128 - turn, 1) if turn else piece)
                keep = lanes < 128 - turn
                rest = pieces[1] if len(pieces) == 2 else jnp.where(keep, pieces[1], pieces[2])
                rows = slice(k * all_ops + at, k * all_ops + at + count_ops)
                flat0[rows, :] = jnp.where(keep, pieces[0], pieces[1])
                flat1[rows, :] = jnp.where(lanes < NCOEF - 128, rest, 0.0)

    for copy in ops_in:
        copy.wait()
    align_rows(range(ROWS_FIRST))

    for copy in rs:
        copy.wait()
    mine = part[me]
    for r in range(1, n_list):
        mine = mine + rs_buf[r - 1]
    multi[me] = mine.astype(BF16)
    ag = []
    for r in far_first:
        copy = pltpu.make_async_remote_copy(
            src_ref=multi.at[me],
            dst_ref=multi.at[me],
            send_sem=ag_send.at[r - 1],
            recv_sem=ag_recv.at[r - 1],
            device_id=(me_leaf, peers[r - 1]),
            device_id_type=MESH,
        )
        copy.start()
        ag.append(copy)

    align_rows(range(ROWS_FIRST, NCOEF))

    def take_op(g, _):
        cols = pl.multiple_of(g * WIDE, WIDE)
        m_cat[:, pl.ds(cols, 128)] = flat0[pl.ds(g, ROWS, stride=all_ops), :].astype(BF16)
        m_cat[:, pl.ds(cols + 128, 128)] = flat1[pl.ds(g, ROWS, stride=all_ops), :].astype(BF16)
        return 0

    lax.fori_loop(0, OPS_FIRST, take_op, 0, unroll=4)

    for copy in cells_in:
        copy.wait()
    for k in range(NEAR):
        pickers[:, k * CAP : k * CAP + CAP] = hot16(let_send[k : k + 1, :], 0, LEAF)
    for copy in ag:
        copy.wait()
    leaves = multi[...].reshape(n_list * CHUNK, LEAF)[:ROWS]
    table[0] = leaves

    picked = dot(leaves, pickers[...]).astype(BF16)
    halo = []
    for k in (0, 7, 1, 6, 2, 5, 3, 4):
        outgoing[k] = picked[:, k * CAP : k * CAP + CAP]
        to = NEAR - 1 - k
        copy = pltpu.make_async_remote_copy(
            src_ref=outgoing.at[k],
            dst_ref=table.at[1 + to // 2, :, to % 2 * CAP : to % 2 * CAP + CAP],
            send_sem=halo_send.at[k],
            recv_sem=halo_recv.at[k],
            device_id=(near_ids[k], me),
            device_id_type=MESH,
        )
        copy.start()
        halo.append(copy)

    lax.fori_loop(OPS_FIRST, n_ops, take_op, 0, unroll=4)
    for copy in lists_in:
        copy.wait()

    def sources(g):
        rows = []
        for v in range(PAIR):
            src = list_src[pl.ds(g + v, 1), :]
            rows.append(jnp.where(iota((1, BATCH), 1) < batch_count[0, g + v], src, TILES * LEAF))
        return jnp.concatenate(rows, axis=1)

    def gather_own(p, _):
        x_own[p] = dot(leaves, hot16(sources(p * PAIR), 0, LEAF)).astype(BF16)
        return 0

    lax.fori_loop(0, n_ops // PAIR, gather_own, 0, unroll=4)
    for copy in halo:
        copy.wait()

    def gather(i):
        for u in range(0, BLOCK, PAIR):
            src = sources(i * BLOCK + u)
            tile = src // LEAF
            others = table[1:].reshape((TILES - 1) * ROWS, LEAF)
            each = dot(others, hot16(src - tile * LEAF, 0, LEAF))
            x = x_own[i * (BLOCK // PAIR) + u // PAIR].astype(F32)
            for h in range(1, TILES):
                x = jnp.where(tile == h, each[(h - 1) * ROWS : h * ROWS], x)
            for v in range(PAIR):
                x_buf[lax.rem(i, 2), u + v] = x[:, v * BATCH : v * BATCH + BATCH].astype(BF16)

    def scatter(i):
        for u in range(BLOCK):
            dst = list_dst[pl.ds(i * BLOCK + u, 1), :]
            z = dot_nt(x_buf[lax.rem(i, 2), u], hot16(dst, 0, LEAF))
            z_buf[lax.rem(i, 2), u * WIDE : u * WIDE + ROWS, :] = z.astype(BF16)

    def apply(i):
        cols = pl.ds(pl.multiple_of(i * (BLOCK * WIDE), BLOCK * WIDE), BLOCK * WIDE)
        total[...] += dot(m_cat[:, cols], z_buf[lax.rem(i, 2)])

    blocks = n_ops // BLOCK
    total[...] = jnp.zeros_like(total)
    z_buf[...] = jnp.zeros_like(z_buf)
    gather(jnp.int32(0))
    scatter(jnp.int32(0))
    gather(jnp.int32(1))

    def steps(i, _):
        apply(i - 2)
        scatter(i - 1)
        gather(i)
        return 0

    lax.fori_loop(2, blocks, steps, 0)
    apply(jnp.int32(blocks - 2))
    scatter(jnp.int32(blocks - 1))
    apply(jnp.int32(blocks - 1))

    left = iota((HALF, 128), 1) < 64
    for j in range(n_list):
        cols = slice(j // 2 * 128, j // 2 * 128 + 128)
        top, low = total[:HALF, cols], total[HALF:, cols]
        if j % 2 == 0:
            fin[j] = jnp.where(left, top, pltpu.roll(low, 64, 1))
        else:
            fin[j] = jnp.where(left, pltpu.roll(top, 64, 1), low)
    last = []
    for r in far_first:
        copy = pltpu.make_async_remote_copy(
            src_ref=fin.at[peers[r - 1]],
            dst_ref=fin_buf.at[r - 1],
            send_sem=fin_send.at[r - 1],
            recv_sem=fin_recv.at[r - 1],
            device_id=(me_leaf, peers[r - 1]),
            device_id_type=MESH,
        )
        copy.start()
        last.append(copy)
    for o in range(OCT):
        rows = pl.ds(n_ops + o, ROWS, stride=all_ops)
        s_cat[:, o * WIDE : o * WIDE + 128] = flat0[rows, :].astype(BF16)
        s_cat[:, o * WIDE + 128 : o * WIDE + 256] = flat1[rows, :].astype(BF16)

    pick[...] = jnp.zeros_like(pick)
    child = iota((128, LEAF), 1)
    cell = iota((128, LEAF), 0)
    octs = octant[pl.ds(0, LEAF)].reshape(1, LEAF)
    for o in range(OCT):
        chosen = onehot(cell == jnp.where(octs == o, child // 8, -1))
        pick[o * WIDE : o * WIDE + ROWS, :] = dot_nt(leaves, chosen).astype(BF16)
    parents = dot(s_cat[...], pick[...]).astype(BF16)
    n_par = LEAF // 8
    child = iota((128, n_par), 1)
    cell = iota((128, n_par), 0)
    octs = octant[pl.ds(LEAF, n_par)].reshape(1, n_par)
    for o in range(OCT):
        chosen = onehot(cell == jnp.where(octs == o, n_par + child // 8, -1))
        pick[o * WIDE : o * WIDE + ROWS, :] = dot_nt(parents[:, :n_par], chosen).astype(BF16)
    grand = dot(s_cat[...], pick[...])
    tree = jnp.where(iota((ROWS, 128), 1) < n_par, parents.astype(F32), grand)
    tree_out[...] = tree.T[:TREE, :NCOEF].astype(BF16)
    tree_done = pltpu.make_async_copy(tree_out, tree_hbm, in_sem.at[9 + IN_PARTS])
    tree_done.start()


    for copy in last:
        copy.wait()
    s = fin[me]
    for r in range(1, n_list):
        s = s + fin_buf[r - 1]
    s = jnp.concatenate([s, pltpu.roll(s, 64, 1)], axis=0)
    local_out[...] = s.T[: local_out.shape[0], :NCOEF].astype(BF16)
    tree_done.wait()


def finish(local, tree, local_out, tree_out):
    local_out[...] = local[...]
    tree_out[...] = tree[: tree_out.shape[0], :]


def per_device(
    n_leaf,
    n_list,
    charge,
    position,
    charge_count,
    octant,
    shift_ops,
    m2l_ops,
    let_send,
    list_src,
    list_dst,
    batch_count,
):
    slots = charge.shape[0]
    n_ops = m2l_ops.shape[0]
    all_ops = SPREAD
    vmem = pl.BlockSpec(memory_space=pltpu.VMEM)
    dma = pltpu.SemaphoreType.DMA
    hbm = pl.BlockSpec(memory_space=pl.ANY)
    local, tree = pl.pallas_call(
        functools.partial(kernel, n_leaf, n_list),
        out_shape=(
            jax.ShapeDtypeStruct((LEAF // n_list, NCOEF), BF16),
            jax.ShapeDtypeStruct((TREE, NCOEF), BF16),
        ),
        in_specs=[hbm] * 10,
        out_specs=(vmem, hbm),
        scratch_shapes=[
            pltpu.VMEM(charge.shape, F32),
            pltpu.VMEM(position.shape, F32),
            pltpu.VMEM((1, LEAF), jnp.int32),
            pltpu.VMEM(octant.shape, jnp.int32),
            pltpu.VMEM(let_send.shape[1:], jnp.int32),
            pltpu.SMEM(batch_count.shape, jnp.int32),
            pltpu.VMEM((TREE, NCOEF), BF16),
            pltpu.VMEM(shift_ops.shape, BF16),
            pltpu.VMEM(m2l_ops.shape, BF16),
            pltpu.VMEM(list_src.shape[1:], jnp.int32),
            pltpu.VMEM(list_src.shape[1:], jnp.int32),
            pltpu.VMEM((ORDER + 1, slots, LEAF), F32),
            pltpu.VMEM((ORDER + 1, slots, LEAF), F32),
            pltpu.VMEM((ORDER + 1, slots, LEAF), F32),
            pltpu.VMEM((LEAF // 128, n_list * CHUNK * 8, 128), F32),
            pltpu.VMEM((n_list, CHUNK, LEAF), F32),
            pltpu.VMEM((n_list - 1, CHUNK, LEAF), F32),
            pltpu.VMEM((n_list, CHUNK, LEAF), BF16),
            pltpu.VMEM((LEAF, NEAR * CAP), BF16),
            pltpu.VMEM((NEAR, ROWS, CAP), BF16),
            pltpu.VMEM((TILES, ROWS, LEAF), BF16),
            pltpu.VMEM((ROWS * all_ops, 128), F32),
            pltpu.VMEM((ROWS * all_ops, 128), F32),
            pltpu.VMEM((ROWS, n_ops * WIDE), BF16),
            pltpu.VMEM((ROWS, OCT * WIDE), BF16),
            pltpu.VMEM((OCT * WIDE, 128), BF16),
            pltpu.VMEM((n_ops // PAIR, ROWS, PAIR * BATCH), BF16),
            pltpu.VMEM((2, BLOCK, ROWS, BATCH), BF16),
            pltpu.VMEM((2, BLOCK * WIDE, LEAF), BF16),
            pltpu.VMEM((ROWS, LEAF), F32),
            pltpu.VMEM((n_list, HALF, 128), F32),
            pltpu.VMEM((n_list - 1, HALF, 128), F32),
            dma((n_list - 1,)),
            dma((n_list - 1,)),
            dma((n_list - 1,)),
            dma((n_list - 1,)),
            dma((NEAR,)),
            dma((NEAR,)),
            dma((n_list - 1,)),
            dma((n_list - 1,)),
            dma((10 + IN_PARTS,)),
        ],
        compiler_params=pltpu.CompilerParams(
            collective_id=0, has_side_effects=True, vmem_limit_bytes=56 << 20
        ),
    )(
        charge,
        position,
        charge_count.reshape(1, -1),
        octant,
        shift_ops,
        m2l_ops,
        let_send[0],
        list_src[0],
        list_dst[0],
        batch_count,
    )
    local_t, tree_t = pl.pallas_call(
        finish,
        out_shape=(
            jax.ShapeDtypeStruct((LEAF // n_list, NCOEF), BF16),
            jax.ShapeDtypeStruct((LEAF // 8 + LEAF // 64, NCOEF), BF16),
        ),
        in_specs=[vmem, vmem],
        out_specs=(vmem, vmem),
    )(local, tree)
    return local_t.T, tree_t.T


def solution(mesh):
    return jax.shard_map(
        functools.partial(per_device, mesh.shape["leaf"], mesh.shape["list"]),
        mesh=mesh,
        in_specs=(
            P("list", "leaf"),
            P(None, "list", "leaf"),
            P("leaf"),
            P("leaf"),
            P(),
            P("list", None),
            P("leaf", None, None),
            P("leaf", "list", None),
            P("leaf", "list", None),
            P("leaf", "list"),
        ),
        out_specs=(P(None, ("leaf", "list")), P(None, "leaf")),
        check_vma=False,
    )
```
